256 devices in a mesh: pts: 32 (over z, y_hi, core), lts: 8 (over y_lo, x).
Axes of the slice: x: 4, y: 4 (y_hi: 2, y_lo: 2; y = y_hi * 2 + y_lo), z: 8, core: 2. Of those that a mesh axis runs over, the one named last changes fastest.
Arguments:
- normals: float32 [3, 8192], P(None, 'pts'), may hold values from -1 to 1, as said below
- view_index: int32 [8192], P('pts'), may hold values from 0 to 63
- cam_dirs: float32 [3, 64], replicated, may hold values from -1 to 1, as said below
- albedo: float32 [3, 8192], P(None, 'pts'), may hold values from 0.05 to 0.95
- roughness: float32 [8192], P('pts'), may hold values from 0.3 to 0.9
- point_feat: float32 [32, 8192], P(None, 'pts'), may hold values from -6 to 6
- observed: float32 [3, 8192], P(None, 'pts'), may hold values from 0 to 1.5
- texel_feat: float32 [32, 32768], P(None, 'lts'), may hold values from -6 to 6
- env: float32 [3, 32768], P(None, 'lts'), may hold values from 0.1 to 10
Outputs:
- radiance: float32 [3, 8192], P(None, 'pts')
- grad_albedo: float32 [3, 8192], P(None, 'pts')
- grad_roughness: float32 [8192], P('pts')
- grad_point_feat: float32 [32, 8192], P(None, 'pts')
- light_step: float32 [3, 32768], P(None, 'lts')
- feat_step: float32 [32, 32768], P(None, 'lts')
The draws below stay inside these ranges and needn't reach their ends.
Inputs may be any that keep to these rules, and one draw needn't show every extreme that they name: `normals`: each column is a unit vector. `cam_dirs`: each column is a unit vector.
All inputs are finite; a program needn't handle non-finite values.
Results may differ from the reference program's by a relative error of at most 0.0003.
Values sent between devices are 32-bit elements; how exact they have to be, the bound alone decides.
No kernel may reach another device: no remote copies, remote signals or barrier semaphores. Data moves between devices by JAX's collectives and lax.ppermute only.
A program may use at most 64 MiB of HBM per device.

```python
import math
import jax
import jax.numpy as jnp
from jax import lax

ROWS = 128
COLS = 256
FEAT = 32
CAMS = 64
POINTS = 8192
TEX = 32768


def unit_columns(key, count, lift):
    raw = jax.random.normal(key, (3, count), jnp.float32)
    raw = raw + lift * (jnp.arange(3) == 2).astype(jnp.float32)[:, None]
    return raw / jnp.sqrt(jnp.sum(raw * raw, axis=0, keepdims=True) + 1e-12)


def draw_normals(key, part):
    key = jax.random.fold_in(key, 1)
    return unit_columns(key, POINTS, 0.0)


def draw_cam_dirs(key, part):
    key = jax.random.fold_in(key, 2)
    return unit_columns(key, CAMS, 0.5)


def with_ends(result, stream_key, smallest, high):
    extent = result.shape
    place = [jax.random.randint(jax.random.fold_in(stream_key, axis), (), 0, extent[axis]) for axis in range(len(extent))]
    result = result.at[tuple(place)].set(smallest)
    longest = extent.index(max(extent))
    place[longest] = (place[longest] + 1) % extent[longest]
    return result.at[tuple(place)].set(high)


def block_scale(own_key, shape, cuts, low, largest):
    level = 1.0
    for dim, shards_of in cuts:
        heights = jax.random.uniform(jax.random.fold_in(jax.random.fold_in(own_key, 6), dim), (shards_of,), jnp.float32, low / len(cuts), largest / len(cuts))
        level = level * jnp.repeat(jnp.exp(heights), shape[dim] // shards_of).reshape((-1,) + (1,) * (len(shape) - 1 - dim))
    return level


def centred(rng, extent, scale, reach, cuts=(), kind=jnp.bfloat16):
    drawn = scale * jax.random.normal(rng, extent, jnp.float32)
    if cuts:
        drawn = drawn * block_scale(rng, extent, cuts, -0.22, 0.18)
    return jnp.clip(drawn, -reach, reach).astype(kind)


def setup_inputs(seed: int = 0) -> dict:
    key_list = jax.random.split(jax.random.key(seed), 10)
    return {
        "normals": draw_normals(jax.random.fold_in(key_list[9], 71), 0),
        "view_index": with_ends(jax.random.randint(key_list[1], (POINTS,), 0, CAMS), jax.random.fold_in(key_list[1], 1), 0, CAMS - 1).astype(jnp.int32),
        "cam_dirs": draw_cam_dirs(jax.random.fold_in(key_list[9], 71), 0),
        "albedo": jnp.clip(0.05 + 0.9 * jax.random.uniform(key_list[3], (3, POINTS), jnp.float32) ** block_scale(key_list[3], (3, POINTS), ((1, 32),), -0.2, 0.2), 0.05, 0.95),
        "roughness": jnp.clip(0.3 + 0.59999996 * jax.random.uniform(key_list[4], (POINTS,), jnp.float32) ** block_scale(key_list[4], (POINTS,), ((0, 32),), -0.2, 0.2), 0.3, 0.9),
        "point_feat": centred(key_list[5], (FEAT, POINTS), 1.0, 6.0, ((1, 32),), jnp.float32),
        "observed": jnp.clip(1.5 * jax.random.uniform(key_list[6], (3, POINTS), jnp.float32) ** block_scale(key_list[6], (3, POINTS), ((1, 32),), -0.2, 0.2), 0.0, 1.5),
        "texel_feat": centred(key_list[7], (FEAT, TEX), 1.0, 6.0, ((1, 8),), jnp.float32),
        "env": jnp.clip(jnp.exp(math.log(10.0) - 4.6051702 * jax.random.uniform(key_list[8], (3, TEX), jnp.float32) ** block_scale(key_list[8], (3, TEX), ((1, 8),), -0.2, 0.2)), 0.1, 10.0),
    }


PRECISE = lax.Precision.HIGHEST

def texel_geometry(start, count):
    texel_pos = start + jnp.arange(count, dtype=jnp.int32)
    row_pos = (texel_pos // COLS).astype(jnp.float32)
    col_pos = (texel_pos % COLS).astype(jnp.float32)
    theta = math.pi * (row_pos + 0.5) / ROWS
    azimuth = 2.0 * math.pi * (col_pos + 0.5) / COLS
    sine = jnp.sin(theta)
    directions = jnp.stack([sine * jnp.cos(azimuth), sine * jnp.sin(azimuth), jnp.cos(theta)])
    weights = sine * (0.5 * math.pi)
    return (directions, weights)

def visibility_score(point_block, texel_block):
    return jnp.einsum('fp,fl->pl', point_block, texel_block, precision=PRECISE) / math.sqrt(point_block.shape[0])

def lobe_kernel(albedo, rough, score, lights, normals, views, directions, weights):
    cos_light = jnp.einsum('kp,kl->pl', normals, directions, precision=PRECISE)
    cos_view = jnp.einsum('kp,kl->pl', views, directions, precision=PRECISE)
    normal_view = lax.optimization_barrier(jnp.sum(normals * views, axis=0))
    view_floor = jnp.maximum(normal_view, 0.1)
    lit = jnp.maximum(cos_light, 0.0)
    half_len = jnp.sqrt(jnp.maximum(2.0 + 2.0 * cos_view, 0.5))
    normal_half = (cos_light + normal_view[:, None]) / half_len
    view_half = (1.0 + cos_view) / half_len
    alpha = rough * rough
    alpha_sq = (alpha * alpha)[:, None]
    denom = normal_half * normal_half * (alpha_sq - 1.0) + 1.0
    distrib = alpha_sq / (math.pi * denom * denom)
    half_rough = (alpha * 0.5)[:, None]
    fresnel = 0.04 + 0.96 * (1.0 - view_half) ** 5
    shadow = (lit * (1.0 - half_rough) + half_rough) * (view_floor[:, None] * (1.0 - half_rough) + half_rough)
    specular = distrib * fresnel / (4.0 * shadow)
    base = jax.nn.sigmoid(score) * lit * weights[None, :]
    contrib = (albedo[:, :, None] / math.pi + specular[None]) * base[None] * lights[:, None, :]
    shaded = 4.0 * math.pi / (ROWS * COLS) * lax.optimization_barrier(jnp.sum(contrib, axis=2))
    energy = lax.optimization_barrier(jnp.sum(contrib * contrib, axis=1))
    return (shaded, energy)

def reference(normals, view_index, cam_dirs, albedo, roughness, point_feat, observed, texel_feat, env):
    choose = (jnp.arange(CAMS, dtype=jnp.int32)[:, None] == view_index[None, :]).astype(jnp.float32)
    views = jnp.dot(cam_dirs, choose, precision=PRECISE, preferred_element_type=jnp.float32)
    directions, weights = texel_geometry(0, TEX)
    width = min(128, POINTS)
    blocks = POINTS // width

    def split(array):
        return array.reshape(array.shape[0], blocks, width).transpose(1, 0, 2)

    def unsplit(array):
        return array.transpose(1, 0, 2).reshape(array.shape[1], POINTS)
    rough_blocks = roughness.reshape(blocks, width)

    def forward(pieces):
        nrm, vws, alb, rgh, feats = pieces
        score = visibility_score(feats, texel_feat)
        shaded, energy = lobe_kernel(alb, rgh, score, env, nrm, vws, directions, weights)
        return shaded
    shaded = lax.map(forward, (split(normals), split(views), split(albedo), rough_blocks, split(point_feat)))
    radiance = unsplit(shaded)
    resid = split(radiance - observed)

    def backward(carry, pieces):
        grad_env, grad_texel, energy_sum = carry
        nrm, vws, alb, rgh, feats, rsd = pieces
        score = visibility_score(feats, texel_feat)

        def local(alb_in, rgh_in, score_in, env_in):
            return lobe_kernel(alb_in, rgh_in, score_in, env_in, nrm, vws, directions, weights)
        shaded_now, pull, energy = jax.vjp(local, alb, rgh, score, env, has_aux=True)
        grad_alb, grad_rgh, grad_score, grad_light = pull(rsd)
        grad_feat = jnp.einsum('fl,pl->fp', texel_feat, grad_score, precision=PRECISE) / math.sqrt(FEAT)
        grad_tex = jnp.einsum('fp,pl->fl', feats, grad_score, precision=PRECISE) / math.sqrt(FEAT)
        carry_next = (grad_env + grad_light, grad_texel + grad_tex, energy_sum + energy)
        return (carry_next, (grad_alb, grad_rgh, grad_feat))
    init = (jnp.zeros((3, TEX), jnp.float32), jnp.zeros((FEAT, TEX), jnp.float32), jnp.zeros((3, TEX), jnp.float32))
    pieces = (split(normals), split(views), split(albedo), rough_blocks, split(point_feat), resid)
    (grad_env, grad_texel, energy_sum), (grad_alb, grad_rgh, grad_feat) = lax.scan(backward, init, pieces)
    grad_albedo = unsplit(grad_alb)
    grad_roughness = grad_rgh.reshape(POINTS)
    grad_point_feat = unsplit(grad_feat)
    scale = TEX / (4.0 * math.pi)
    light_step = env * grad_env * scale / jnp.sqrt(energy_sum + 1e-06 * POINTS)
    total_energy = lax.optimization_barrier(jnp.sum(energy_sum, axis=0, keepdims=True))
    feat_step = grad_texel * scale / jnp.sqrt(total_energy + 3e-06 * POINTS)
    return (radiance, grad_albedo, grad_roughness, grad_point_feat, light_step, feat_step)
```

```python
import functools
import math

import jax
import jax.numpy as jnp
import numpy as np
from jax import lax
from jax.experimental import pallas as pl
from jax.experimental.pallas import tpu as pltpu
from jax.sharding import PartitionSpec as P

ROWS = 128
COLS = 256
F32 = jnp.float32
BF16 = jnp.bfloat16

THETA = np.pi * (np.arange(ROWS) + 0.5) / ROWS
PHI = 2.0 * np.pi * (np.arange(COLS) + 0.5) / COLS
THETA_TABLE = np.stack([np.sin(THETA), np.cos(THETA)]).astype(np.float32)
PHI_TABLE = np.stack([np.cos(PHI), np.sin(PHI)]).astype(np.float32)

PTS = 256
BLK = 256
CHUNK = 16
(NZ, VZ, NV0, AM1, KEEP, KOFF, C1, C0, YA, YD, YG) = range(11)
NCONST = 11

TN = (((0,), (0,)), ((), ()))
NT = (((1,), (1,)), ((), ()))
NN = (((1,), (0,)), ((), ()))


def dot(a, b, dims):
    return lax.dot_general(a, b, dims, preferred_element_type=F32)


def split(x):
    hi = x.astype(BF16)
    return hi, (x - hi.astype(F32)).astype(BF16)


def shade_kernel(
    theta_ref,
    phi_ref,
    normals_ref,
    view_ref,
    cams_ref,
    albedo_ref,
    rough_ref,
    pfeat_ref,
    tfeat_ref,
    env_ref,
    bh_ref,
    bl_ref,
    sh_ref,
    sl_ref,
    qbh_ref,
    qbl_ref,
    qsh_ref,
    qsl_ref,
    sums_ref,
    fb_ref,
    fs_ref,
    energy_ref,
    const,
    azim_n,
    azim_v,
    pfs,
    score,
    yh,
    yl,
    squares,
    amat,
    ebuf,
    acc_s,
    acc_fb,
    acc_fs,
):
    step = pl.program_id(0)
    row = lax.axis_index("lts") * pl.num_programs(0) + step
    sin_t = theta_ref[0, row]
    cos_t = theta_ref[1, row]

    @pl.when(step == 0)
    def prologue():
        normals = normals_ref[...]
        cams = lax.broadcasted_iota(jnp.int32, (cams_ref.shape[1], PTS), 0)
        choose = (cams == view_ref[...]).astype(F32)
        views = lax.dot_general(
            cams_ref[...], choose, NN, precision=lax.Precision.HIGHEST, preferred_element_type=F32
        )
        rough = rough_ref[...]
        alpha = rough * rough
        alpha_sq = alpha * alpha
        half = 0.5 * alpha
        nv0 = jnp.sum(normals * views, axis=0, keepdims=True)
        nv = jnp.maximum(nv0, 0.1)
        geo_v = nv * (1.0 - half) + half
        lead = alpha_sq / (4.0 * math.pi * geo_v)
        y_d = -4.0 * alpha / (1.0 - alpha_sq)
        y_g = -0.5 / (1.0 - half)
        y_a = 2.0 / alpha - y_d - y_g - (1.0 - nv) / (2.0 * geo_v)
        two_r = 2.0 * rough
        rows = [None] * NCONST
        rows[NZ] = normals[2:3]
        rows[VZ] = 0.5 * views[2:3]
        rows[NV0] = nv0
        rows[AM1] = 0.25 * (alpha_sq - 1.0)
        rows[KEEP] = 1.0 - half
        rows[KOFF] = half
        rows[C1] = 0.96 * lead
        rows[C0] = 0.04 * lead
        rows[YA] = two_r * y_a
        rows[YD] = two_r * y_d
        rows[YG] = two_r * y_g
        rows += [normals[0:1], normals[1:2], 0.5 * views[0:1], 0.5 * views[1:2]]
        for k, r in enumerate(rows):
            ebuf[k : k + 1, :] = r
        cols = ebuf[...].T
        for k in range(NCONST):
            const[k] = jnp.broadcast_to(cols[:, k : k + 1], (PTS, 128))
        cos_p = phi_ref[0:1, :]
        sin_p = phi_ref[1:2, :]
        k = NCONST
        azim_n[...] = cols[:, k : k + 1] * cos_p + cols[:, k + 1 : k + 2] * sin_p
        azim_v[...] = cols[:, k + 2 : k + 3] * cos_p + cols[:, k + 3 : k + 4] * sin_p
        hi, lo = split((pfeat_ref[...] * (0.5 / math.sqrt(pfeat_ref.shape[0]))).T)
        pfs[:, 0:32] = hi
        pfs[:, 32:64] = lo
        pfs[:, 64:96] = hi
        ebuf[...] = jnp.zeros_like(ebuf)
        alb = albedo_ref[...] * (1.0 / math.pi)
        for j, a in enumerate((alb * alb, 2.0 * alb)):
            hi = a.astype(BF16).astype(F32)
            ebuf[0:3, :] = hi
            ebuf[3:6, :] = a - hi
            amat[:, j * PTS : (j + 1) * PTS] = ebuf[0:16, :].astype(BF16)
        ebuf[0:3, :] = jnp.ones((3, PTS), F32)
        ebuf[3:6, :] = jnp.zeros((3, PTS), F32)
        amat[:, 2 * PTS : 3 * PTS] = ebuf[0:16, :].astype(BF16)
        acc_s[...] = jnp.zeros_like(acc_s)
        acc_fb[...] = jnp.zeros_like(acc_fb)
        acc_fs[...] = jnp.zeros_like(acc_fs)

    tfeat = tfeat_ref[...]
    t_hi, t_lo = split(tfeat)
    score[...] = dot(pfs[...], jnp.concatenate([t_hi, t_hi, t_lo], axis=0), NN)

    def chunk(i, carry):
        r0 = pl.multiple_of(i * CHUNK, CHUNK)
        rows = pl.ds(r0, CHUNK)
        c = [const[k, rows, :] for k in range(NCONST)]
        nz = c[NZ] * cos_t
        vz = c[VZ] * cos_t + 0.5
        for h in range(BLK // 128):
            lanes = pl.ds(h * 128, 128)
            nl = azim_n[rows, lanes] * sin_t + nz
            vv = azim_v[rows, lanes] * sin_t + vz
            tt = jnp.tanh(score[rows, lanes])
            lit = jnp.maximum(nl, 0.0)
            inv_len = lax.rsqrt(jnp.maximum(vv, 0.125))
            nh = (nl + c[NV0]) * inv_len
            dd = nh * nh * c[AM1] + 1.0
            gg = lit * c[KEEP] + c[KOFF]
            dg = dd * gg
            inv = pl.reciprocal(dd * dg, approx=True)
            x1 = 1.0 - vv * inv_len
            x2 = x1 * x1
            fres = x2 * x2 * x1 * c[C1] + c[C0]
            base = (1.0 + tt) * lit
            spec = fres * inv * base
            fact = inv * dd * (c[YD] * gg + c[YG] * dd) + c[YA]
            yy = spec * fact
            rest = 1.0 - tt
            qb = base * rest
            qs = spec * rest
            for x, hi_ref, lo_ref in (
                (base, bh_ref, bl_ref),
                (spec, sh_ref, sl_ref),
                (qb, qbh_ref, qbl_ref),
                (qs, qsh_ref, qsl_ref),
                (yy, yh, yl),
            ):
                hi, lo = split(x)
                hi_ref[rows, lanes] = hi
                lo_ref[rows, lanes] = lo
            squares[pl.ds(r0, CHUNK), lanes] = (base * base).astype(BF16)
            squares[pl.ds(PTS + r0, CHUNK), lanes] = (base * spec).astype(BF16)
            squares[pl.ds(2 * PTS + r0, CHUNK), lanes] = (spec * spec).astype(BF16)
        return carry

    lax.fori_loop(0, PTS // CHUNK, chunk, 0)

    light = env_ref[...] * (sin_t * (0.25 * math.pi))
    l_hi = light.astype(BF16).astype(F32)
    ebuf[0:3, :] = l_hi
    ebuf[3:6, :] = light - l_hi
    lmat = ebuf[0:16, :].astype(BF16)
    for k, (hi_ref, lo_ref) in enumerate(((bh_ref, bl_ref), (sh_ref, sl_ref), (yh, yl))):
        acc_s[k] += dot(lmat, hi_ref[...], NT) + dot(lmat, lo_ref[...], NT)
    parts = [split(tfeat * light[k : k + 1]) for k in range(3)]
    f_hi = jnp.concatenate([p[0] for p in parts], axis=0)
    f_all = jnp.concatenate([p[0] for p in parts] + [p[1] for p in parts], axis=0)
    for acc, hi_ref, lo_ref in ((acc_fb, qbh_ref, qbl_ref), (acc_fs, qsh_ref, qsl_ref)):
        acc[...] += dot(f_all, hi_ref[...], NT)
        acc[0:96, :] += dot(f_hi, lo_ref[...], NT)
    eng = dot(amat[...], squares[...], NN)
    energy_ref[...] = light * light * (eng[0:3] + eng[3:6])

    @pl.when(step == pl.num_programs(0) - 1)
    def epilogue():
        for k in range(3):
            sums_ref[3 * k : 3 * k + 3, :] = acc_s[k, 0:3, :] + acc_s[k, 3:6, :]
        fb_ref[...] = acc_fb[0:96, :] + acc_fb[96:192, :]
        fs_ref[...] = acc_fs[0:96, :] + acc_fs[96:192, :]


def grad_kernel(
    scale,
    sums_ref,
    albedo_ref,
    observed_ref,
    pfeat_ref,
    fb_ref,
    fs_ref,
    energy_ref,
    theta_ref,
    env_ref,
    bh_ref,
    bl_ref,
    sh_ref,
    sl_ref,
    qbh_ref,
    qbl_ref,
    qsh_ref,
    qsl_ref,
    point_ref,
    gpf_ref,
    out_ref,
    rbuf,
    rb,
    rs,
    wb,
    ws,
):
    step = pl.program_id(0)
    row = lax.axis_index("lts") * pl.num_programs(0) + step
    sin_t = theta_ref[0, row]
    half_root = 0.5 / math.sqrt(pfeat_ref.shape[0])

    @pl.when(step == 0)
    def prologue():
        sums = sums_ref[...]
        alb = albedo_ref[...] * (1.0 / math.pi)
        radiance = scale * (alb * sums[0:3] + sums[3:6])
        resid = radiance - observed_ref[...]
        resid_a = resid * alb
        point_ref[0:3, :] = radiance
        point_ref[3:6, :] = (scale / math.pi) * resid * sums[0:3]
        point_ref[6:7, :] = scale * jnp.sum(resid * sums[6:9], axis=0, keepdims=True)
        pf = pfeat_ref[...] * half_root
        total = jnp.zeros_like(gpf_ref)
        for k in range(3):
            a = resid_a[k : k + 1]
            r = resid[k : k + 1]
            f = pl.ds(32 * k, 32)
            total += a * fb_ref[f, :] + r * fs_ref[f, :]
            for w_ref, x in ((wb, a), (ws, r)):
                hi, lo = split(pf * x)
                w_ref[pl.ds(32 * k, 32), :] = hi
                w_ref[pl.ds(96 + 32 * k, 32), :] = lo
        gpf_ref[...] = (scale * half_root) * total
        rbuf[...] = jnp.zeros_like(rbuf)
        for w_ref, x in ((rb, resid_a), (rs, resid)):
            hi = x.astype(BF16).astype(F32)
            rbuf[0:3, :] = hi
            rbuf[3:6, :] = x - hi
            w_ref[...] = rbuf[...].astype(BF16)

    light = env_ref[...] * (sin_t * (0.25 * math.pi))
    g = (
        dot(rb[...], bh_ref[...], NN)
        + dot(rb[...], bl_ref[...], NN)
        + dot(rs[...], sh_ref[...], NN)
        + dot(rs[...], sl_ref[...], NN)
    )
    x = dot(wb[...], qbh_ref[...], NN) + dot(ws[...], qsh_ref[...], NN)
    x = x[0:96] + x[96:192]
    x += dot(wb[0:96, :], qbl_ref[...], NN) + dot(ws[0:96, :], qsl_ref[...], NN)
    total = light[0:1] * x[0:32]
    for k in (1, 2):
        total += light[k : k + 1] * x[32 * k : 32 * k + 32]
    out_ref[0:32, :] = total
    out_ref[32:35, :] = light * (g[0:3] + g[3:6])
    out_ref[35:38, :] = energy_ref[...]
    out_ref[38:40, :] = jnp.zeros((2, BLK), F32)


def shards(normals, view_index, cam_dirs, albedo, roughness, point_feat, observed, texel_feat, env):
    pts = normals.shape[1]
    tex = env.shape[1]
    steps = tex // BLK
    points_all = lax.axis_size("pts") * pts
    tex_all = tex * lax.axis_size("lts")
    scale = 4.0 * math.pi / tex_all
    theta = jnp.asarray(THETA_TABLE)
    phi = jnp.asarray(PHI_TABLE)

    def whole(shape):
        return pl.BlockSpec(shape, lambda i: (0,) * len(shape))

    def tile(rows):
        return pl.BlockSpec((rows, BLK), lambda i: (0, i))

    smem = pl.BlockSpec(memory_space=pltpu.SMEM)
    big = jax.ShapeDtypeStruct((pts, tex), BF16)
    outs = pl.pallas_call(
        shade_kernel,
        grid=(steps,),
        in_specs=[
            smem,
            whole((2, COLS)),
            whole((3, pts)),
            whole((1, pts)),
            whole(cam_dirs.shape),
            whole((3, pts)),
            whole((1, pts)),
            whole((32, pts)),
            tile(32),
            tile(3),
        ],
        out_specs=[tile(pts)] * 8 + [whole((9, pts)), whole((96, pts)), whole((96, pts)), tile(3)],
        out_shape=[big] * 8
        + [
            jax.ShapeDtypeStruct((9, pts), F32),
            jax.ShapeDtypeStruct((96, pts), F32),
            jax.ShapeDtypeStruct((96, pts), F32),
            jax.ShapeDtypeStruct((3, tex), F32),
        ],
        scratch_shapes=[
            pltpu.VMEM((NCONST, PTS, 128), F32),
            pltpu.VMEM((PTS, COLS), F32),
            pltpu.VMEM((PTS, COLS), F32),
            pltpu.VMEM((PTS, 96), BF16),
            pltpu.VMEM((PTS, BLK), F32),
            pltpu.VMEM((PTS, BLK), BF16),
            pltpu.VMEM((PTS, BLK), BF16),
            pltpu.VMEM((3 * PTS, BLK), BF16),
            pltpu.VMEM((16, 3 * PTS), BF16),
            pltpu.VMEM((16, BLK), F32),
            pltpu.VMEM((3, 16, PTS), F32),
            pltpu.VMEM((192, PTS), F32),
            pltpu.VMEM((192, PTS), F32),
        ],
        compiler_params=pltpu.CompilerParams(vmem_limit_bytes=24 * 1024 * 1024),
        name="shade",
    )(
        theta,
        phi,
        normals,
        view_index.reshape(1, pts),
        cam_dirs,
        albedo,
        roughness.reshape(1, pts),
        point_feat,
        texel_feat,
        env,
    )
    mats, (sums, fb, fs, energy) = outs[:8], outs[8:]

    def swap(x, axis, bits):
        n = lax.axis_size(axis)
        return lax.ppermute(x, axis, [(i, i ^ bits) for i in range(n)])

    sums = sums + swap(sums, "lts", 4)
    sums = sums + swap(sums, "lts", 1) + swap(sums, "lts", 2) + swap(sums, "lts", 3)

    point_out, gpf, out = pl.pallas_call(
        functools.partial(grad_kernel, scale),
        grid=(steps,),
        in_specs=[
            whole((9, pts)),
            whole((3, pts)),
            whole((3, pts)),
            whole((32, pts)),
            whole((96, pts)),
            whole((96, pts)),
            tile(3),
            smem,
            tile(3),
        ]
        + [tile(pts)] * 8,
        out_specs=[whole((8, pts)), whole((32, pts)), tile(40)],
        out_shape=[
            jax.ShapeDtypeStruct((8, pts), F32),
            jax.ShapeDtypeStruct((32, pts), F32),
            jax.ShapeDtypeStruct((40, tex), F32),
        ],
        scratch_shapes=[
            pltpu.VMEM((16, PTS), F32),
            pltpu.VMEM((16, PTS), BF16),
            pltpu.VMEM((16, PTS), BF16),
            pltpu.VMEM((192, PTS), BF16),
            pltpu.VMEM((192, PTS), BF16),
        ],
        compiler_params=pltpu.CompilerParams(vmem_limit_bytes=24 * 1024 * 1024),
        name="grads",
    )(sums, albedo, observed, point_feat, fb, fs, energy, theta, env, *mats)

    gpf = gpf + swap(gpf, "lts", 4)
    gpf = gpf + swap(gpf, "lts", 1) + swap(gpf, "lts", 2) + swap(gpf, "lts", 3)

    place = lax.axis_index("pts")

    def halve(x, bit):
        n = x.shape[1] // 2
        lo, hi = x[:, :n], x[:, n:]
        low = (place & bit) == 0
        return jnp.where(low, lo, hi) + swap(jnp.where(low, hi, lo), "pts", bit)

    def double(x, bit):
        other = swap(x, "pts", bit)
        low = (place & bit) == 0
        return jnp.concatenate([jnp.where(low, x, other), jnp.where(low, other, x)], axis=1)

    x = out
    for bit in (1, 4, 8):
        x = halve(x, bit)
    for bit in (16, 2):
        x = x + swap(x, "pts", bit)
    light_step = x[32:35] * lax.rsqrt(x[35:38] + 1e-06 * points_all)
    total = jnp.sum(x[35:38], axis=0, keepdims=True)
    feat_step = x[0:32] * lax.rsqrt(total + 3e-06 * points_all)
    x = jnp.concatenate([feat_step, light_step], axis=0)
    for bit in (8, 4, 1):
        x = double(x, bit)
    return (point_out[0:3], point_out[3:6], point_out[6], gpf, x[32:35], x[0:32])


def solution(mesh):
    return jax.shard_map(
        shards,
        mesh=mesh,
        in_specs=(
            P(None, "pts"),
            P("pts"),
            P(),
            P(None, "pts"),
            P("pts"),
            P(None, "pts"),
            P(None, "pts"),
            P(None, "lts"),
            P(None, "lts"),
        ),
        out_specs=(
            P(None, "pts"),
            P(None, "pts"),
            P("pts"),
            P(None, "pts"),
            P(None, "lts"),
            P(None, "lts"),
        ),
        check_vma=False,
    )
```

```python
import functools
import math

import jax
import jax.numpy as jnp
import numpy as np
from jax import lax
from jax.experimental import pallas as pl
from jax.experimental.pallas import tpu as pltpu
from jax.sharding import PartitionSpec as P

ROWS = 128
COLS = 256
F32 = jnp.float32
BF16 = jnp.bfloat16

THETA = np.pi * (np.arange(ROWS) + 0.5) / ROWS
PHI = 2.0 * np.pi * (np.arange(COLS) + 0.5) / COLS
THETA_TABLE = np.stack([np.sin(THETA), np.cos(THETA)]).astype(np.float32)
PHI_TABLE = np.stack([np.cos(PHI), np.sin(PHI)]).astype(np.float32)

PTS = 256
BLK = 256
CHUNK = 16
UNROLL = 16
(NZ, VZ, NV0, AM1, KEEP, KOFF, C1, C0, YA, YD, YG, ALB) = range(12)
NCONST = 14

NT = (((1,), (1,)), ((), ()))
NN = (((1,), (0,)), ((), ()))


def dot(a, b, dims):
    return lax.dot_general(a, b, dims, preferred_element_type=F32)


def split(x):
    hi = x.astype(BF16)
    return hi, (x - hi.astype(F32)).astype(BF16)


def score_tile(pfs_ref, tfeat):
    t_hi, t_lo = split(tfeat)
    return dot(pfs_ref[...], jnp.concatenate([t_hi, t_hi, t_lo], axis=0), NN)


def fold(x):
    return x[0:8] + x[8:16]


def shade_kernel(
    theta_ref,
    phi_ref,
    normals_ref,
    view_ref,
    cams_ref,
    albedo_ref,
    rough_ref,
    pfeat_ref,
    tfeat_ref,
    env_ref,
    spec_ref,
    sums_ref,
    energy_ref,
    azim_n,
    pfs,
    nz_ref,
    const,
    azim_v,
    score_a,
    score_b,
    mats_a,
    mats_b,
    ebuf,
    acc,
    spec_buf,
    sems,
):
    steps = tfeat_ref.shape[1] // BLK
    first = lax.axis_index("lts") * steps

    def prologue():
        normals = normals_ref[...]
        cams = lax.broadcasted_iota(jnp.int32, (cams_ref.shape[1], PTS), 0)
        choose = (cams == view_ref[...]).astype(F32)
        views = lax.dot_general(
            cams_ref[...], choose, NN, precision=lax.Precision.HIGHEST, preferred_element_type=F32
        )
        rough = rough_ref[...]
        alpha = rough * rough
        alpha_sq = alpha * alpha
        half = 0.5 * alpha
        nv0 = jnp.sum(normals * views, axis=0, keepdims=True)
        nv = jnp.maximum(nv0, 0.1)
        geo_v = nv * (1.0 - half) + half
        lead = alpha_sq / (4.0 * math.pi * geo_v)
        y_d = -4.0 * alpha / (1.0 - alpha_sq)
        y_g = -0.5 / (1.0 - half)
        y_a = 2.0 / alpha - y_d - y_g - (1.0 - nv) / (2.0 * geo_v)
        two_r = 2.0 * rough
        rows = [None] * NCONST
        rows[NZ] = normals[2:3]
        rows[VZ] = 0.5 * views[2:3]
        rows[NV0] = nv0
        rows[AM1] = 0.25 * (alpha_sq - 1.0)
        rows[KEEP] = 1.0 - half
        rows[KOFF] = half
        rows[C1] = 0.96 * lead
        rows[C0] = 0.04 * lead
        rows[YA] = two_r * y_a
        rows[YD] = two_r * y_d
        rows[YG] = two_r * y_g
        for k in range(3):
            rows[ALB + k] = albedo_ref[k : k + 1, :] * (1.0 / math.pi)
        rows += [normals[0:1], normals[1:2], 0.5 * views[0:1], 0.5 * views[1:2]]
        ebuf[...] = jnp.zeros_like(ebuf)
        for k, r in enumerate(rows):
            ebuf[k : k + 1, :] = r
        cols = ebuf[...].T
        for k in range(NCONST):
            const[k] = jnp.broadcast_to(cols[:, k : k + 1], (PTS, 128))
        nz_ref[...] = const[NZ]
        cos_p = phi_ref[0:1, :]
        sin_p = phi_ref[1:2, :]
        k = NCONST
        azim_n[...] = cols[:, k : k + 1] * cos_p + cols[:, k + 1 : k + 2] * sin_p
        azim_v[...] = cols[:, k + 2 : k + 3] * cos_p + cols[:, k + 3 : k + 4] * sin_p
        hi, lo = split((pfeat_ref[...] * (0.5 / math.sqrt(pfeat_ref.shape[0]))).T)
        pfs[:, 0:32] = hi
        pfs[:, 32:64] = lo
        pfs[:, 64:96] = hi
        ebuf[...] = jnp.zeros_like(ebuf)
        acc[...] = jnp.zeros_like(acc)

    prologue()
    mats_b[...] = jnp.zeros_like(mats_b)

    def place(step):
        return pl.ds(pl.multiple_of(step * BLK, BLK), BLK)

    def light_of(step):
        return env_ref[:, place(step)] * (theta_ref[0, first + step] * (0.25 * math.pi))

    def spec_copy(step):
        return pltpu.make_async_copy(spec_buf.at[step], spec_ref.at[step], sems.at[step])

    def shade(step, score, mats):
        sin_t = theta_ref[0, first + step]
        cos_t = theta_ref[1, first + step]
        light = light_of(step)

        def chunk(i, eng):
            r0 = pl.multiple_of(i * CHUNK, CHUNK)
            rows = pl.ds(r0, CHUNK)
            c = [const[k, rows, :] for k in range(NCONST)]
            nz = c[NZ] * cos_t
            vz = c[VZ] * cos_t + 0.5
            eng = list(eng)
            for h in range(BLK // 128):
                lanes = pl.ds(h * 128, 128)
                nl = azim_n[rows, lanes] * sin_t + nz
                vv = azim_v[rows, lanes] * sin_t + vz
                tt = jnp.tanh(score[rows, lanes])
                lit = jnp.maximum(nl, 0.0)
                inv_len = lax.rsqrt(jnp.maximum(vv, 0.125))
                nh = (nl + c[NV0]) * inv_len
                dd = nh * nh * c[AM1] + 1.0
                gg = lit * c[KEEP] + c[KOFF]
                inv = pl.reciprocal(dd * dd * gg, approx=True)
                x1 = 1.0 - vv * inv_len
                x2 = x1 * x1
                fres = x2 * x2 * x1 * c[C1] + c[C0]
                base = (1.0 + tt) * lit
                spec = fres * inv * base
                fact = inv * dd * (c[YD] * gg + c[YG] * dd) + c[YA]
                spec_buf[step, rows, lanes] = spec
                for k, x in enumerate((base, spec, spec * fact)):
                    hi, lo = split(x)
                    mats[pl.ds(2 * k * PTS + r0, CHUNK), lanes] = hi
                    mats[pl.ds((2 * k + 1) * PTS + r0, CHUNK), lanes] = lo
                for k in range(3):
                    v = c[ALB + k] * base + spec
                    eng[3 * h + k] += fold(v * v)
            return tuple(eng)

        zero = jnp.zeros((8, 128), F32)
        eng = lax.fori_loop(0, PTS // CHUNK, chunk, (zero,) * 6, unroll=UNROLL)
        for h in range(BLK // 128):
            for k in range(3):
                lk = light[k : k + 1, 128 * h : 128 * h + 128]
                energy_ref[k : k + 1, pl.ds(pl.multiple_of(step * BLK + 128 * h, 128), 128)] = lk * lk * jnp.sum(eng[3 * h + k], axis=0, keepdims=True)

        spec_copy(step).start()

    def contract(step, mats):
        light = light_of(step)
        l_hi = light.astype(BF16).astype(F32)
        ebuf[0:3, :] = l_hi
        ebuf[3:6, :] = light - l_hi
        acc[...] += dot(ebuf[0:16, :].astype(BF16), mats[...], NT)

    score_a[...] = score_tile(pfs, tfeat_ref[:, place(0)])

    @pl.loop(0, steps // 2)
    def pair(j):
        a = 2 * j
        score_b[...] = score_tile(pfs, tfeat_ref[:, place(a + 1)])
        shade(a, score_a, mats_a)
        contract(jnp.maximum(a - 1, 0), mats_b)
        score_a[...] = score_tile(pfs, tfeat_ref[:, place(jnp.minimum(a + 2, steps - 1))])
        shade(a + 1, score_b, mats_b)
        contract(a, mats_a)

    contract(steps - 1, mats_b)
    both = acc[0:3, :] + acc[3:6, :]
    for k in range(3):
        at = 2 * k * PTS
        sums_ref[3 * k : 3 * k + 3, :] = both[:, at : at + PTS] + both[:, at + PTS : at + 2 * PTS]

    @pl.loop(0, steps)
    def drain(step):
        spec_copy(step).wait()


def grad_kernel(
    scale,
    half,
    theta_ref,
    p0_ref,
    p1_ref,
    p2_ref,
    p3_ref,
    albedo_ref,
    observed_ref,
    pfeat_ref,
    azim_n,
    pfs,
    nz_ref,
    tfeat_ref,
    env_ref,
    spec_ref,
    energy_ref,
    before_ref,
    point_ref,
    gpf_ref,
    out_ref,
    const,
    rbuf,
    wmat,
    score_a,
    score_b,
    d_a,
    d_b,
    acc,
    spec_buf,
    sems,
):
    tiles = tfeat_ref.shape[1] // BLK
    steps = tiles // 2
    core = lax.axis_index("pts") % 2
    base_tile = (core if half else 1 - core) * steps
    first = lax.axis_index("lts") * tiles + base_tile
    half_root = 0.5 / math.sqrt(pfeat_ref.shape[0])

    def prologue():
        sums = (p0_ref[...] + p1_ref[...]) + (p2_ref[...] + p3_ref[...])
        alb = albedo_ref[...] * (1.0 / math.pi)
        radiance = scale * (alb * sums[0:3] + sums[3:6])
        resid = radiance - observed_ref[...]
        point_ref[0:3, :] = radiance
        point_ref[3:6, :] = (scale / math.pi) * resid * sums[0:3]
        point_ref[6:7, :] = scale * jnp.sum(resid * sums[6:9], axis=0, keepdims=True)
        rbuf[...] = jnp.zeros_like(rbuf)
        rbuf[0:3, :] = resid * alb
        rbuf[3:6, :] = resid
        cols = rbuf[...].T
        for k in range(6):
            const[k] = jnp.broadcast_to(cols[:, k : k + 1], (PTS, 128))
        hi, lo = split(pfeat_ref[...] * half_root)
        wmat[0:32, :] = hi
        wmat[32:64, :] = lo
        acc[...] = jnp.zeros_like(acc)

    def spec_copy(step):
        return pltpu.make_async_copy(
            spec_ref.at[base_tile + step], spec_buf.at[step], sems.at[step]
        )

    @pl.loop(0, steps)
    def fetch(step):
        spec_copy(step).start()

    prologue()
    mine = pl.ds(pl.multiple_of(base_tile * BLK, BLK), steps * BLK)
    out_ref[35:38, :] = energy_ref[:, mine]
    out_ref[38:40, :] = jnp.zeros((2, steps * BLK), F32)
    d_b[...] = jnp.zeros_like(d_b)

    def place(step):
        return pl.ds(pl.multiple_of(step * BLK, BLK), BLK)

    def tfeat_of(step):
        return tfeat_ref[:, place(base_tile + step)]

    def combine(step, score, d):
        sin_t = theta_ref[0, first + step]
        cos_t = theta_ref[1, first + step]
        light = env_ref[:, place(base_tile + step)] * (sin_t * (0.25 * math.pi))
        spec_copy(step).wait()

        def chunk(i, gain):
            r0 = pl.multiple_of(i * CHUNK, CHUNK)
            rows = pl.ds(r0, CHUNK)
            c = [const[k, rows, :] for k in range(6)]
            nz = nz_ref[rows, :] * cos_t
            gain = list(gain)
            for h in range(BLK // 128):
                lanes = pl.ds(h * 128, 128)
                tt = jnp.tanh(score[rows, lanes])
                lit = jnp.maximum(azim_n[rows, lanes] * sin_t + nz, 0.0)
                base = (1.0 + tt) * lit
                spec = spec_buf[step, rows, lanes]
                total = None
                for k in range(3):
                    v = c[k] * base + c[3 + k] * spec
                    gain[3 * h + k] += fold(v)
                    lv = light[k : k + 1, 128 * h : 128 * h + 128] * v
                    total = lv if total is None else total + lv
                hi, lo = split(total * (1.0 - tt))
                d[0, rows, lanes] = hi
                d[1, rows, lanes] = lo
            return tuple(gain)

        zero = jnp.zeros((8, 128), F32)
        gain = lax.fori_loop(0, PTS // CHUNK, chunk, (zero,) * 6, unroll=UNROLL)
        for h in range(BLK // 128):
            for k in range(3):
                lk = light[k : k + 1, 128 * h : 128 * h + 128]
                out_ref[32 + k : 33 + k, pl.ds(pl.multiple_of(step * BLK + 128 * h, 128), 128)] = lk * jnp.sum(gain[3 * h + k], axis=0, keepdims=True)

    def contract(step, d):
        dh = d[0]
        dl = d[1]
        x = dot(wmat[...], dh, NN)
        out_ref[0:32, place(step)] = x[0:32] + x[32:64] + dot(wmat[0:32, :], dl, NN)
        t_hi, t_lo = split(tfeat_of(step))
        acc[...] += dot(jnp.concatenate([t_hi, t_lo], axis=0), dh, NT)
        acc[0:32, :] += dot(t_hi, dl, NT)

    score_a[...] = score_tile(pfs, tfeat_of(0))

    @pl.loop(0, steps // 2)
    def pair(j):
        a = 2 * j
        score_b[...] = score_tile(pfs, tfeat_of(a + 1))
        combine(a, score_a, d_a)
        contract(jnp.maximum(a - 1, 0), d_b)
        score_a[...] = score_tile(pfs, tfeat_of(jnp.minimum(a + 2, steps - 1)))
        combine(a + 1, score_b, d_b)
        contract(a, d_a)

    contract(steps - 1, d_b)
    gpf_ref[...] = before_ref[...] + (scale * half_root) * (acc[0:32, :] + acc[32:64, :])


def add(*arrays):
    def body(*refs):
        total = refs[0][...]
        for ref in refs[1:-1]:
            total += ref[...]
        refs[-1][...] = total

    shape = jax.ShapeDtypeStruct(arrays[0].shape, F32)
    return pl.pallas_call(body, out_shape=shape, name="add")(*arrays)


def shards(normals, view_index, cam_dirs, albedo, roughness, point_feat, observed, texel_feat, env):
    pts = normals.shape[1]
    tex = env.shape[1]
    steps = tex // BLK
    points_all = lax.axis_size("pts") * pts
    tex_all = tex * lax.axis_size("lts")
    scale = 4.0 * math.pi / tex_all
    theta = jnp.asarray(THETA_TABLE)
    phi = jnp.asarray(PHI_TABLE)

    vmem = pl.BlockSpec(memory_space=pltpu.VMEM)
    smem = pl.BlockSpec(memory_space=pltpu.SMEM)
    params = pltpu.CompilerParams(vmem_limit_bytes=60 * 1024 * 1024)

    def shape(*dims, dtype=F32):
        return jax.ShapeDtypeStruct(dims, dtype)

    spec, sums, energy, azim_n, pfs, nz = pl.pallas_call(
        shade_kernel,
        in_specs=[smem] + [vmem] * 9,
        out_specs=[pl.BlockSpec(memory_space=pl.ANY)] + [vmem] * 5,
        out_shape=[
            shape(steps, pts, BLK),
            shape(9, pts),
            shape(3, tex),
            shape(pts, COLS),
            shape(pts, 96, dtype=BF16),
            shape(pts, 128),
        ],
        scratch_shapes=[
            pltpu.VMEM((NCONST, PTS, 128), F32),
            pltpu.VMEM((PTS, COLS), F32),
            pltpu.VMEM((PTS, BLK), F32),
            pltpu.VMEM((PTS, BLK), F32),
            pltpu.VMEM((6 * PTS, BLK), BF16),
            pltpu.VMEM((6 * PTS, BLK), BF16),
            pltpu.VMEM((24, BLK), F32),
            pltpu.VMEM((16, 6 * PTS), F32),
            pltpu.VMEM((steps, PTS, BLK), F32),
            pltpu.SemaphoreType.DMA((steps,)),
        ],
        compiler_params=params,
        name="shade",
    )(
        theta,
        phi,
        normals,
        view_index.reshape(1, pts),
        cam_dirs,
        albedo,
        roughness.reshape(1, pts),
        point_feat,
        texel_feat,
        env,
    )

    def swap(x, axis, bits):
        n = lax.axis_size(axis)
        return lax.ppermute(x, axis, [(i, i ^ bits) for i in range(n)])

    sums = sums + swap(sums, "lts", 4)
    parts = [sums] + [swap(sums, "lts", k) for k in (1, 2, 3)]

    def grads(half, before):
        anywhere = pl.BlockSpec(memory_space=pl.ANY)
        return pl.pallas_call(
            functools.partial(grad_kernel, scale, half),
            in_specs=[smem] + [vmem] * 12 + [anywhere] + [vmem] * 2,
            out_specs=[vmem] * 3,
            out_shape=[shape(8, pts), shape(32, pts), shape(40, tex // 2)],
            scratch_shapes=[
                pltpu.VMEM((6, PTS, 128), F32),
                pltpu.VMEM((8, PTS), F32),
                pltpu.VMEM((64, PTS), BF16),
                pltpu.VMEM((PTS, BLK), F32),
                pltpu.VMEM((PTS, BLK), F32),
                pltpu.VMEM((2, PTS, BLK), BF16),
                pltpu.VMEM((2, PTS, BLK), BF16),
                pltpu.VMEM((64, PTS), F32),
                pltpu.VMEM((steps // 2, PTS, BLK), F32),
                pltpu.SemaphoreType.DMA((steps // 2,)),
            ],
            compiler_params=params,
            name="grads" + str(half),
        )(
            theta,
            *parts,
            albedo,
            observed,
            point_feat,
            azim_n,
            pfs,
            nz,
            texel_feat,
            env,
            spec,
            energy,
            before,
        )

    place = lax.axis_index("pts")
    barrier = lax.optimization_barrier
    _, gpf, other = grads(0, jnp.zeros((32, pts), F32))
    other = swap(other, "pts", 1)
    point_out, gpf, own = grads(1, gpf)

    quad = tex // 8
    group = (place >> 1) & 3
    mask = (8, 16, 24)
    x = own + other
    gpf_other = swap(gpf, "lts", 4)
    cut = [lax.dynamic_slice(x, (0, quad * (group ^ m)), (40, quad)) for m in range(4)]
    gpf, *cut = barrier((gpf + gpf_other, *cut))
    got = [swap(cut[m], "pts", 2 * m) for m in (1, 2, 3)]
    gpf_got = [swap(gpf, "lts", m) for m in (1, 2, 3)]
    x = (cut[0] + got[0]) + (got[1] + got[2])
    gpf = (gpf + gpf_got[0]) + (gpf_got[1] + gpf_got[2])
    x, gpf = barrier((x, gpf))
    got = [swap(x, "pts", m) for m in mask]
    x = (x + got[0]) + (got[1] + got[2])
    light_step = x[32:35] * lax.rsqrt(x[35:38] + 1e-06 * points_all)
    total = jnp.sum(x[35:38], axis=0, keepdims=True)
    feat_step = x[0:32] * lax.rsqrt(total + 3e-06 * points_all)
    x = jnp.concatenate([feat_step, light_step], axis=0)
    got = [x] + [swap(x, "pts", 2 * m) for m in (1, 2, 3)]
    pieces = []
    for j in range(4):
        k = group ^ j
        low = jnp.where(k == 0, got[0], got[1])
        pieces.append(jnp.where(k < 2, low, jnp.where(k == 2, got[2], got[3])))
    x = jnp.concatenate(pieces, axis=1)
    other = swap(x, "pts", 1)
    low = (place & 1) == 0
    x = jnp.concatenate([jnp.where(low, x, other), jnp.where(low, other, x)], axis=1)
    return (point_out[0:3], point_out[3:6], point_out[6], gpf, x[32:35], x[0:32])


def solution(mesh):
    return jax.shard_map(
        shards,
        mesh=mesh,
        in_specs=(
            P(None, "pts"),
            P("pts"),
            P(),
            P(None, "pts"),
            P("pts"),
            P(None, "pts"),
            P(None, "pts"),
            P(None, "lts"),
            P(None, "lts"),
        ),
        out_specs=(
            P(None, "pts"),
            P(None, "pts"),
            P("pts"),
            P(None, "pts"),
            P(None, "lts"),
            P(None, "lts"),
        ),
        check_vma=False,
    )
```

```python
import functools
import math

import jax
import jax.numpy as jnp
import numpy as np
from jax import lax
from jax.experimental import pallas as pl
from jax.experimental.pallas import tpu as pltpu
from jax.sharding import PartitionSpec as P

ROWS = 128
COLS = 256
F32 = jnp.float32
BF16 = jnp.bfloat16

THETA = np.pi * (np.arange(ROWS) + 0.5) / ROWS
PHI = 2.0 * np.pi * (np.arange(COLS) + 0.5) / COLS
THETA_TABLE = np.stack([np.sin(THETA), np.cos(THETA)]).astype(np.float32)
PHI_TABLE = np.stack([np.cos(PHI), np.sin(PHI)]).astype(np.float32)

PTS = 256
BLK = 256
CHUNK = 16
UNROLL = 16
(NZ, VZ, NV0, AM1, KEEP, KOFF, C1, C0, YA, YD, YG, ALB) = range(12)
NCONST = 14

NT = (((1,), (1,)), ((), ()))
NN = (((1,), (0,)), ((), ()))


def dot(a, b, dims):
    return lax.dot_general(a, b, dims, preferred_element_type=F32)


def split(x):
    hi = x.astype(BF16)
    return hi, (x - hi.astype(F32)).astype(BF16)


def score_tile(pfs_ref, tfeat):
    t_hi, t_lo = split(tfeat)
    return dot(pfs_ref[...], jnp.concatenate([t_hi, t_hi, t_lo], axis=0), NN)


def fold(x):
    return x[0:8] + x[8:16]


def shade_kernel(
    theta_ref,
    phi_ref,
    normals_ref,
    view_ref,
    cams_ref,
    albedo_ref,
    rough_ref,
    pfeat_ref,
    tfeat_ref,
    env_ref,
    spec_ref,
    sums_ref,
    energy_ref,
    azim_n,
    pfs,
    nz_ref,
    const,
    azim_v,
    score_a,
    score_b,
    mats_a,
    mats_b,
    ebuf,
    acc,
    acc_rad,
    spec_buf,
    sems,
):
    steps = tfeat_ref.shape[1] // BLK
    first = lax.axis_index("lts") * steps

    def prologue():
        normals = normals_ref[...]
        cams = lax.broadcasted_iota(jnp.int32, (cams_ref.shape[1], PTS), 0)
        choose = (cams == view_ref[...]).astype(F32)
        views = lax.dot_general(
            cams_ref[...], choose, NN, precision=lax.Precision.HIGHEST, preferred_element_type=F32
        )
        rough = rough_ref[...]
        alpha = rough * rough
        alpha_sq = alpha * alpha
        half = 0.5 * alpha
        nv0 = jnp.sum(normals * views, axis=0, keepdims=True)
        nv = jnp.maximum(nv0, 0.1)
        geo_v = nv * (1.0 - half) + half
        lead = alpha_sq / (4.0 * math.pi * geo_v)
        y_d = -4.0 * alpha / (1.0 - alpha_sq)
        y_g = -0.5 / (1.0 - half)
        y_a = 2.0 / alpha - y_d - y_g - (1.0 - nv) / (2.0 * geo_v)
        two_r = 2.0 * rough
        rows = [None] * NCONST
        rows[NZ] = normals[2:3]
        rows[VZ] = 0.5 * views[2:3]
        rows[NV0] = nv0
        rows[AM1] = 0.25 * (alpha_sq - 1.0)
        rows[KEEP] = 1.0 - half
        rows[KOFF] = half
        rows[C1] = 0.96 * lead
        rows[C0] = 0.04 * lead
        rows[YA] = two_r * y_a
        rows[YD] = two_r * y_d
        rows[YG] = two_r * y_g
        for k in range(3):
            rows[ALB + k] = albedo_ref[k : k + 1, :] * (1.0 / math.pi)
        rows += [normals[0:1], normals[1:2], 0.5 * views[0:1], 0.5 * views[1:2]]
        ebuf[...] = jnp.zeros_like(ebuf)
        for k, r in enumerate(rows):
            ebuf[k : k + 1, :] = r
        cols = ebuf[...].T
        for k in range(NCONST):
            const[k] = jnp.broadcast_to(cols[:, k : k + 1], (PTS, 128))
        nz_ref[...] = const[NZ]
        cos_p = phi_ref[0:1, :]
        sin_p = phi_ref[1:2, :]
        k = NCONST
        azim_n[...] = cols[:, k : k + 1] * cos_p + cols[:, k + 1 : k + 2] * sin_p
        azim_v[...] = cols[:, k + 2 : k + 3] * cos_p + cols[:, k + 3 : k + 4] * sin_p
        hi, lo = split((pfeat_ref[...] * (0.5 / math.sqrt(pfeat_ref.shape[0]))).T)
        pfs[:, 0:32] = hi
        pfs[:, 32:64] = lo
        pfs[:, 64:96] = hi
        ebuf[...] = jnp.zeros_like(ebuf)
        acc[...] = jnp.zeros_like(acc)
        acc_rad[...] = jnp.zeros_like(acc_rad)

    prologue()
    mats_b[...] = jnp.zeros_like(mats_b)

    def place(step):
        return pl.ds(pl.multiple_of(step * BLK, BLK), BLK)

    def light_of(step):
        return env_ref[:, place(step)] * (theta_ref[0, first + step] * (0.25 * math.pi))

    def spec_copy(step):
        return pltpu.make_async_copy(spec_buf.at[step], spec_ref.at[step], sems.at[step])

    def shade(step, score, mats):
        sin_t = theta_ref[0, first + step]
        cos_t = theta_ref[1, first + step]
        light = light_of(step)

        def chunk(i, eng):
            r0 = pl.multiple_of(i * CHUNK, CHUNK)
            rows = pl.ds(r0, CHUNK)
            c = [const[k, rows, :] for k in range(NCONST)]
            nz = c[NZ] * cos_t
            vz = c[VZ] * cos_t + 0.5
            eng = list(eng)
            rad = [None] * 3
            for h in range(BLK // 128):
                lanes = pl.ds(h * 128, 128)
                nl = azim_n[rows, lanes] * sin_t + nz
                vv = azim_v[rows, lanes] * sin_t + vz
                tt = jnp.tanh(score[rows, lanes])
                lit = jnp.maximum(nl, 0.0)
                inv_len = lax.rsqrt(jnp.maximum(vv, 0.125))
                nh = (nl + c[NV0]) * inv_len
                dd = nh * nh * c[AM1] + 1.0
                gg = lit * c[KEEP] + c[KOFF]
                inv = pl.reciprocal(dd * dd * gg, approx=True)
                x1 = 1.0 - vv * inv_len
                x2 = x1 * x1
                fres = x2 * x2 * x1 * c[C1] + c[C0]
                base = (1.0 + tt) * lit
                spec = fres * inv * base
                fact = inv * dd * (c[YD] * gg + c[YG] * dd) + c[YA]
                spec_buf[step, rows, lanes] = spec
                hi, lo = split(spec * fact)
                mats[pl.ds(r0, CHUNK), lanes] = base.astype(BF16)
                mats[pl.ds(PTS + r0, CHUNK), lanes] = hi
                mats[pl.ds(2 * PTS + r0, CHUNK), lanes] = lo
                for k in range(3):
                    v = c[ALB + k] * base + spec
                    eng[3 * h + k] += fold(v * v)
                    lv = light[k : k + 1, 128 * h : 128 * h + 128] * v
                    rad[k] = lv if h == 0 else rad[k] + lv
            for k in range(3):
                acc_rad[k, rows, :] += rad[k]
            return tuple(eng)

        zero = jnp.zeros((8, 128), F32)
        eng = lax.fori_loop(0, PTS // CHUNK, chunk, (zero,) * 6, unroll=UNROLL)
        for h in range(BLK // 128):
            for k in range(3):
                lk = light[k : k + 1, 128 * h : 128 * h + 128]
                energy_ref[k : k + 1, pl.ds(pl.multiple_of(step * BLK + 128 * h, 128), 128)] = lk * lk * jnp.sum(eng[3 * h + k], axis=0, keepdims=True)

        spec_copy(step).start()

    def contract(step, mats):
        light = light_of(step)
        l_hi = light.astype(BF16).astype(F32)
        ebuf[0:3, :] = l_hi
        ebuf[3:6, :] = light - l_hi
        acc[...] += dot(ebuf[0:16, :].astype(BF16), mats[...], NT)

    score_a[...] = score_tile(pfs, tfeat_ref[:, place(0)])

    @pl.loop(0, steps // 2)
    def pair(j):
        a = 2 * j
        score_b[...] = score_tile(pfs, tfeat_ref[:, place(a + 1)])
        shade(a, score_a, mats_a)
        contract(jnp.maximum(a - 1, 0), mats_b)
        score_a[...] = score_tile(pfs, tfeat_ref[:, place(jnp.minimum(a + 2, steps - 1))])
        shade(a + 1, score_b, mats_b)
        contract(a, mats_a)

    contract(steps - 1, mats_b)
    both = acc[0:3, :] + acc[3:6, :]
    rows = [both[:, 0:PTS], both[:, PTS : 2 * PTS] + both[:, 2 * PTS : 3 * PTS]]
    for k in range(3):
        const[0, :, k : k + 1] = jnp.sum(acc_rad[k], axis=1, keepdims=True)
    rows.append(const[0].T[0:3, :])
    for j in range(sums_ref.shape[0]):
        for k in range(3):
            sums_ref[j, 3 * k : 3 * k + 3, :] = rows[k]

    @pl.loop(0, steps)
    def drain(step):
        spec_copy(step).wait()


def grad_kernel(
    scale,
    half,
    theta_ref,
    sums_ref,
    albedo_ref,
    observed_ref,
    pfeat_ref,
    azim_n,
    pfs,
    nz_ref,
    tfeat_ref,
    env_ref,
    spec_ref,
    energy_ref,
    before_ref,
    rad_ref,
    galb_ref,
    grough_ref,
    gpf_ref,
    out_ref,
    const,
    rbuf,
    wmat,
    score_a,
    score_b,
    d_a,
    d_b,
    acc,
    spec_buf,
    sems,
):
    tiles = tfeat_ref.shape[1] // BLK
    steps = tiles // 2
    core = lax.axis_index("pts") % 2
    base_tile = (core if half else 1 - core) * steps
    first = lax.axis_index("lts") * tiles + base_tile
    half_root = 0.5 / math.sqrt(pfeat_ref.shape[0])

    def prologue():
        sums = sums_ref[0]
        for k in range(1, sums_ref.shape[0]):
            sums += sums_ref[k]
        alb = albedo_ref[...] * (1.0 / math.pi)
        radiance = scale * sums[6:9]
        resid = radiance - observed_ref[...]
        rad_ref[...] = radiance
        galb_ref[...] = (scale / math.pi) * resid * sums[0:3]
        grough_ref[...] = scale * jnp.sum(resid * sums[3:6], axis=0, keepdims=True)
        rbuf[...] = jnp.zeros_like(rbuf)
        rbuf[0:3, :] = resid * alb
        rbuf[3:6, :] = resid
        cols = rbuf[...].T
        for k in range(6):
            const[k] = jnp.broadcast_to(cols[:, k : k + 1], (PTS, 128))
        hi, lo = split(pfeat_ref[...] * half_root)
        wmat[0:32, :] = hi
        wmat[32:64, :] = lo
        acc[...] = jnp.zeros_like(acc)

    def spec_copy(step):
        return pltpu.make_async_copy(
            spec_ref.at[base_tile + step], spec_buf.at[step], sems.at[step]
        )

    @pl.loop(0, steps)
    def fetch(step):
        spec_copy(step).start()

    prologue()
    mine = pl.ds(pl.multiple_of(base_tile * BLK, BLK), steps * BLK)
    out_ref[35:38, :] = energy_ref[:, mine]
    out_ref[38:40, :] = jnp.zeros((2, steps * BLK), F32)
    d_b[...] = jnp.zeros_like(d_b)

    def place(step):
        return pl.ds(pl.multiple_of(step * BLK, BLK), BLK)

    def tfeat_of(step):
        return tfeat_ref[:, place(base_tile + step)]

    def combine(step, score, d):
        sin_t = theta_ref[0, first + step]
        cos_t = theta_ref[1, first + step]
        light = env_ref[:, place(base_tile + step)] * (sin_t * (0.25 * math.pi))
        spec_copy(step).wait()

        def chunk(i, gain):
            r0 = pl.multiple_of(i * CHUNK, CHUNK)
            rows = pl.ds(r0, CHUNK)
            c = [const[k, rows, :] for k in range(6)]
            nz = nz_ref[rows, :] * cos_t
            gain = list(gain)
            for h in range(BLK // 128):
                lanes = pl.ds(h * 128, 128)
                tt = jnp.tanh(score[rows, lanes])
                lit = jnp.maximum(azim_n[rows, lanes] * sin_t + nz, 0.0)
                base = (1.0 + tt) * lit
                spec = spec_buf[step, rows, lanes]
                total = None
                for k in range(3):
                    v = c[k] * base + c[3 + k] * spec
                    gain[3 * h + k] += fold(v)
                    lv = light[k : k + 1, 128 * h : 128 * h + 128] * v
                    total = lv if total is None else total + lv
                hi, lo = split(total * (1.0 - tt))
                d[0, rows, lanes] = hi
                d[1, rows, lanes] = lo
            return tuple(gain)

        zero = jnp.zeros((8, 128), F32)
        gain = lax.fori_loop(0, PTS // CHUNK, chunk, (zero,) * 6, unroll=UNROLL)
        for h in range(BLK // 128):
            for k in range(3):
                lk = light[k : k + 1, 128 * h : 128 * h + 128]
                out_ref[32 + k : 33 + k, pl.ds(pl.multiple_of(step * BLK + 128 * h, 128), 128)] = lk * jnp.sum(gain[3 * h + k], axis=0, keepdims=True)

    def contract(step, d):
        dh = d[0]
        dl = d[1]
        x = dot(wmat[...], dh, NN)
        out_ref[0:32, place(step)] = x[0:32] + x[32:64] + dot(wmat[0:32, :], dl, NN)
        t_hi, t_lo = split(tfeat_of(step))
        acc[...] += dot(jnp.concatenate([t_hi, t_lo], axis=0), dh, NT)
        acc[0:32, :] += dot(t_hi, dl, NT)

    score_a[...] = score_tile(pfs, tfeat_of(0))

    @pl.loop(0, steps // 2)
    def pair(j):
        a = 2 * j
        score_b[...] = score_tile(pfs, tfeat_of(a + 1))
        combine(a, score_a, d_a)
        contract(jnp.maximum(a - 1, 0), d_b)
        score_a[...] = score_tile(pfs, tfeat_of(jnp.minimum(a + 2, steps - 1)))
        combine(a + 1, score_b, d_b)
        contract(a, d_a)

    contract(steps - 1, d_b)
    gpf = (scale * half_root) * (acc[0:32, :] + acc[32:64, :])
    gpf_ref[...] = gpf + before_ref[...] if half else gpf


def join_kernel(own_ref, other_ref, feat_ref, light_ref):
    core = lax.axis_index("pts") % 2
    count = own_ref.shape[1]
    for x_ref, at in ((own_ref, core), (other_ref, 1 - core)):
        lanes = pl.ds(pl.multiple_of(at * count, count), count)
        feat_ref[:, lanes] = x_ref[0:32, :]
        light_ref[:, lanes] = x_ref[32:35, :]


def join(own, other, tex):
    return pl.pallas_call(
        join_kernel,
        out_shape=[jax.ShapeDtypeStruct((32, tex), F32), jax.ShapeDtypeStruct((3, tex), F32)],
        compiler_params=pltpu.CompilerParams(vmem_limit_bytes=4 * 1024 * 1024),
        name="join",
    )(own, other)


def shards(normals, view_index, cam_dirs, albedo, roughness, point_feat, observed, texel_feat, env):
    pts = normals.shape[1]
    tex = env.shape[1]
    steps = tex // BLK
    points_all = lax.axis_size("pts") * pts
    tex_all = tex * lax.axis_size("lts")
    scale = 4.0 * math.pi / tex_all
    theta = jnp.asarray(THETA_TABLE)
    phi = jnp.asarray(PHI_TABLE)

    vmem = pl.BlockSpec(memory_space=pltpu.VMEM)
    smem = pl.BlockSpec(memory_space=pltpu.SMEM)
    params = pltpu.CompilerParams(vmem_limit_bytes=20 * 1024 * 1024)

    def hbm(x):
        return pltpu.with_memory_space_constraint(x, pltpu.HBM)

    normals, cam_dirs, albedo, point_feat, observed, texel_feat, env, theta, phi = map(
        hbm, (normals, cam_dirs, albedo, point_feat, observed, texel_feat, env, theta, phi)
    )
    view_index, roughness = (hbm(x.reshape(1, pts)) for x in (view_index, roughness))

    def shape(*dims, dtype=F32):
        return jax.ShapeDtypeStruct(dims, dtype)

    spec, sums, energy, azim_n, pfs, nz = pl.pallas_call(
        shade_kernel,
        in_specs=[smem] + [vmem] * 9,
        out_specs=[pl.BlockSpec(memory_space=pl.ANY)] + [vmem] * 5,
        out_shape=[
            pltpu.HBM((steps, pts, BLK), F32),
            shape(lax.axis_size("lts"), 9, pts),
            shape(3, tex),
            shape(pts, COLS),
            shape(pts, 96, dtype=BF16),
            shape(pts, 128),
        ],
        scratch_shapes=[
            pltpu.VMEM((NCONST, PTS, 128), F32),
            pltpu.VMEM((PTS, COLS), F32),
            pltpu.VMEM((PTS, BLK), F32),
            pltpu.VMEM((PTS, BLK), F32),
            pltpu.VMEM((3 * PTS, BLK), BF16),
            pltpu.VMEM((3 * PTS, BLK), BF16),
            pltpu.VMEM((24, BLK), F32),
            pltpu.VMEM((16, 3 * PTS), F32),
            pltpu.VMEM((3, PTS, 128), F32),
            pltpu.VMEM((steps, PTS, BLK), F32),
            pltpu.SemaphoreType.DMA((steps,)),
        ],
        compiler_params=params,
        name="shade",
    )(
        theta,
        phi,
        normals,
        view_index,
        cam_dirs,
        albedo,
        roughness,
        point_feat,
        texel_feat,
        env,
    )

    def swap(x, axis, bits):
        n = lax.axis_size(axis)
        return lax.ppermute(x, axis, [(i, i ^ bits) for i in range(n)])

    spec = hbm(spec)
    sums = lax.all_to_all(sums, "lts", 0, 0)

    def grads(half, *before):
        def kernel(*refs):
            refs = refs if half else refs[:12] + (None,) + refs[12:]
            grad_kernel(scale, half, *refs)

        anywhere = pl.BlockSpec(memory_space=pl.ANY)
        return pl.pallas_call(
            kernel,
            in_specs=[smem] + [vmem] * 9 + [anywhere, vmem] + [vmem] * half,
            out_specs=[vmem] * 5,
            out_shape=[shape(3, pts), shape(3, pts), shape(1, pts), shape(32, pts), shape(40, tex // 2)],
            scratch_shapes=[
                pltpu.VMEM((6, PTS, 128), F32),
                pltpu.VMEM((8, PTS), F32),
                pltpu.VMEM((64, PTS), BF16),
                pltpu.VMEM((PTS, BLK), F32),
                pltpu.VMEM((PTS, BLK), F32),
                pltpu.VMEM((2, PTS, BLK), BF16),
                pltpu.VMEM((2, PTS, BLK), BF16),
                pltpu.VMEM((64, PTS), F32),
                pltpu.VMEM((steps // 2, PTS, BLK), F32),
                pltpu.SemaphoreType.DMA((steps // 2,)),
            ],
            compiler_params=params,
            name="grads" + str(half),
        )(
            theta,
            sums,
            albedo,
            observed,
            point_feat,
            azim_n,
            pfs,
            nz,
            texel_feat,
            env,
            spec,
            energy,
            *before,
        )

    place = lax.axis_index("pts")
    barrier = lax.optimization_barrier
    *_, gpf, other = grads(0)
    other = swap(other, "pts", 1)
    radiance, grad_albedo, grad_rough, gpf, own = grads(1, gpf)

    quad = tex // 8
    group = (place >> 1) & 3
    gpf_other = swap(gpf, "lts", 4)
    x = own + other
    cut = [lax.dynamic_slice(x, (0, quad * (group ^ m)), (40, quad)) for m in range(4)]
    got = [swap(cut[m], "pts", 2 * m) for m in (1, 2, 3)]
    x = (cut[0] + got[0]) + (got[1] + got[2])
    for m, n in ((8, 1), (24, 2)):
        x, gpf_other = barrier((x, gpf_other))
        x_other = swap(x, "pts", m)
        gpf = gpf + gpf_other
        gpf_other = swap(gpf, "lts", n)
        x = x + x_other
    light_step = x[32:35] * lax.rsqrt(x[35:38] + 1e-06 * points_all)
    total = jnp.sum(x[35:38], axis=0, keepdims=True)
    feat_step = x[0:32] * lax.rsqrt(total + 3e-06 * points_all)
    x = jnp.concatenate([feat_step, light_step], axis=0)
    x, gpf_other = barrier((x, gpf_other))
    gpf = gpf + gpf_other
    got = [x] + [swap(x, "pts", 2 * m) for m in (1, 2, 3)]
    pieces = []
    for j in range(4):
        k = group ^ j
        low = jnp.where(k == 0, got[0], got[1])
        pieces.append(jnp.where(k < 2, low, jnp.where(k == 2, got[2], got[3])))
    x = jnp.concatenate(pieces, axis=1)
    other = swap(x, "pts", 1)
    feat_step, light_step = join(x, other, tex)
    return (radiance, grad_albedo, grad_rough.reshape(pts), gpf, light_step, feat_step)


def solution(mesh):
    return jax.shard_map(
        shards,
        mesh=mesh,
        in_specs=(
            P(None, "pts"),
            P("pts"),
            P(),
            P(None, "pts"),
            P("pts"),
            P(None, "pts"),
            P(None, "pts"),
            P(None, "lts"),
            P(None, "lts"),
        ),
        out_specs=(
            P(None, "pts"),
            P(None, "pts"),
            P("pts"),
            P(None, "pts"),
            P(None, "lts"),
            P(None, "lts"),
        ),
        check_vma=False,
    )
```

```python
import functools
import math

import jax
import jax.numpy as jnp
import numpy as np
from jax import lax
from jax.experimental import pallas as pl
from jax.experimental.pallas import tpu as pltpu
from jax.sharding import PartitionSpec as P

ROWS = 128
COLS = 256
F32 = jnp.float32
BF16 = jnp.bfloat16

THETA = np.pi * (np.arange(ROWS) + 0.5) / ROWS
PHI = 2.0 * np.pi * (np.arange(COLS) + 0.5) / COLS
THETA_TABLE = np.stack([np.sin(THETA), np.cos(THETA)]).astype(np.float32)
PHI_TABLE = np.stack([np.cos(PHI), np.sin(PHI)]).astype(np.float32)

PTS = 256
BLK = 256
CHUNK = 32
GRADS_AT = (0, 1, 3, 4)
SUMS_AT = (0, 1, 2, 3, 4, 5)
SUM_ROWS = 128
SCORE_AT = (6, 7)
SCORE_ROWS = 128
(NZ, VZ, NV0, AM1, KEEP, KOFF, C1, C0, YA, YD, YG, ALB) = range(12)
NCONST = 14

NT = (((1,), (1,)), ((), ()))
NN = (((1,), (0,)), ((), ()))


def dot(a, b, dims):
    return lax.dot_general(a, b, dims, preferred_element_type=F32)


def split(x):
    hi = x.astype(BF16)
    return hi, (x - hi.astype(F32)).astype(BF16)


def score_tile(pfs_ref, tfeat):
    t_hi, t_lo = split(tfeat)
    return dot(pfs_ref[...], jnp.concatenate([t_hi, t_hi, t_lo], axis=0), NN)


def fold(x):
    return (x[0:8] + x[8:16]) + (x[16:24] + x[24:32])


def shade_kernel(
    theta_ref,
    phi_ref,
    normals_ref,
    view_ref,
    cams_ref,
    albedo_ref,
    rough_ref,
    pfeat_ref,
    tfeat_ref,
    env_ref,
    spec_ref,
    sums_ref,
    energy_ref,
    azim_n,
    pfs,
    nz_ref,
    const,
    azim_v,
    score_a,
    score_b,
    mats_a,
    mats_b,
    ebuf,
    acc,
    acc_rad,
    spec_buf,
    sems,
):
    steps = tfeat_ref.shape[1] // BLK
    first = lax.axis_index("lts") * steps

    def prologue():
        normals = normals_ref[...]
        cams = lax.broadcasted_iota(jnp.int32, (cams_ref.shape[1], PTS), 0)
        choose = (cams == view_ref[...]).astype(F32)
        views = lax.dot_general(
            cams_ref[...], choose, NN, precision=lax.Precision.HIGHEST, preferred_element_type=F32
        )
        rough = rough_ref[...]
        alpha = rough * rough
        alpha_sq = alpha * alpha
        half = 0.5 * alpha
        nv0 = jnp.sum(normals * views, axis=0, keepdims=True)
        nv = jnp.maximum(nv0, 0.1)
        geo_v = nv * (1.0 - half) + half
        lead = alpha_sq / (4.0 * math.pi * geo_v)
        y_d = -4.0 * alpha / (1.0 - alpha_sq)
        y_g = -0.5 / (1.0 - half)
        y_a = 2.0 / alpha - y_d - y_g - (1.0 - nv) / (2.0 * geo_v)
        two_r = 2.0 * rough
        rows = [None] * NCONST
        rows[NZ] = normals[2:3]
        rows[VZ] = 0.5 * views[2:3]
        rows[NV0] = nv0
        rows[AM1] = 0.25 * (alpha_sq - 1.0)
        rows[KEEP] = 1.0 - half
        rows[KOFF] = half
        rows[C1] = 0.96 * lead
        rows[C0] = 0.04 * lead
        rows[YA] = two_r * y_a
        rows[YD] = two_r * y_d
        rows[YG] = two_r * y_g
        for k in range(3):
            rows[ALB + k] = albedo_ref[k : k + 1, :] * (1.0 / math.pi)
        rows += [normals[0:1], normals[1:2], 0.5 * views[0:1], 0.5 * views[1:2]]
        ebuf[...] = jnp.zeros_like(ebuf)
        for k, r in enumerate(rows):
            ebuf[k : k + 1, :] = r
        cols = ebuf[...].T
        for k in range(NCONST):
            const[k] = jnp.broadcast_to(cols[:, k : k + 1], (PTS, 128))
        nz_ref[...] = const[NZ]
        cos_p = phi_ref[0:1, :]
        sin_p = phi_ref[1:2, :]
        k = NCONST
        azim_n[...] = cols[:, k : k + 1] * cos_p + cols[:, k + 1 : k + 2] * sin_p
        azim_v[...] = cols[:, k + 2 : k + 3] * cos_p + cols[:, k + 3 : k + 4] * sin_p
        hi, lo = split((pfeat_ref[...] * (0.5 / math.sqrt(pfeat_ref.shape[0]))).T)
        pfs[:, 0:32] = hi
        pfs[:, 32:64] = lo
        pfs[:, 64:96] = hi
        ebuf[...] = jnp.zeros_like(ebuf)
        acc[...] = jnp.zeros_like(acc)
        acc_rad[...] = jnp.zeros_like(acc_rad)

    prologue()
    mats_b[...] = jnp.zeros_like(mats_b)

    def place(step):
        return pl.ds(pl.multiple_of(step * BLK, BLK), BLK)

    def light_of(step):
        return env_ref[:, place(step)] * (theta_ref[0, first + step] * (0.25 * math.pi))

    def spec_copy(step):
        return pltpu.make_async_copy(spec_buf.at[step], spec_ref.at[step], sems.at[step])

    def shade(step, score, mats, beside):
        sin_t = theta_ref[0, first + step]
        cos_t = theta_ref[1, first + step]
        light = light_of(step)

        def chunk(i, eng):
            r0 = i * CHUNK
            rows = pl.ds(r0, CHUNK)
            c = [const[k, rows, :] for k in range(NCONST)]
            nz = c[NZ] * cos_t
            vz = c[VZ] * cos_t + 0.5
            eng = list(eng)
            rad = [None] * 3
            for h in range(BLK // 128):
                lanes = pl.ds(h * 128, 128)
                nl = azim_n[rows, lanes] * sin_t + nz
                vv = azim_v[rows, lanes] * sin_t + vz
                tt = jnp.tanh(score[rows, lanes])
                lit = jnp.maximum(nl, 0.0)
                inv_len = lax.rsqrt(jnp.maximum(vv, 0.125))
                nh = (nl + c[NV0]) * inv_len
                dd = nh * nh * c[AM1] + 1.0
                gg = lit * c[KEEP] + c[KOFF]
                inv = pl.reciprocal(dd * dd * gg, approx=True)
                x1 = 1.0 - vv * inv_len
                x2 = x1 * x1
                fres = x2 * x2 * x1 * c[C1] + c[C0]
                base = (1.0 + tt) * lit
                spec = fres * inv * base
                fact = inv * dd * (c[YD] * gg + c[YG] * dd) + c[YA]
                spec_buf[step, rows, lanes] = spec
                hi, lo = split(spec * fact)
                mats[pl.ds(r0, CHUNK), lanes] = base.astype(BF16)
                mats[pl.ds(PTS + r0, CHUNK), lanes] = hi
                mats[pl.ds(2 * PTS + r0, CHUNK), lanes] = lo
                for k in range(3):
                    v = c[ALB + k] * base + spec
                    eng[3 * h + k] += fold(v * v)
                    lv = light[k : k + 1, 128 * h : 128 * h + 128] * v
                    rad[k] = lv if h == 0 else rad[k] + lv
            for k in range(3):
                acc_rad[k, rows, :] += rad[k]
            return tuple(eng)

        eng = (jnp.zeros((8, 128), F32),) * 6
        for i in range(PTS // CHUNK):
            finish = beside(i)
            eng = chunk(i, eng)
            finish()
        for h in range(BLK // 128):
            for k in range(3):
                lk = light[k : k + 1, 128 * h : 128 * h + 128]
                energy_ref[k : k + 1, pl.ds(pl.multiple_of(step * BLK + 128 * h, 128), 128)] = lk * lk * jnp.sum(eng[3 * h + k], axis=0, keepdims=True)

        spec_copy(step).start()

    def light_rows(step):
        light = light_of(step)
        l_hi = light.astype(BF16).astype(F32)
        ebuf[0:3, :] = l_hi
        ebuf[3:6, :] = light - l_hi
        return ebuf[0:16, :].astype(BF16)

    def beside(lmat, mats, score, nxt):
        t_hi, t_lo = split(tfeat_ref[:, place(nxt)])
        feats = jnp.concatenate([t_hi, t_hi, t_lo], axis=0)

        def run(i):
            if i in SUMS_AT:
                part = pl.ds(SUMS_AT.index(i) * SUM_ROWS, SUM_ROWS)
                x = dot(lmat, mats[part, :], NT)

                def finish():
                    acc[:, part] += x

            elif i in SCORE_AT:
                rows = pl.ds(SCORE_AT.index(i) * SCORE_ROWS, SCORE_ROWS)
                x = dot(pfs[rows, :], feats, NN)

                def finish():
                    score[rows, :] = x

            else:

                def finish():
                    pass

            return finish

        return run

    score_a[...] = score_tile(pfs, tfeat_ref[:, place(0)])

    @pl.loop(0, steps // 2)
    def pair(j):
        a = 2 * j
        lmat = light_rows(jnp.maximum(a - 1, 0))
        shade(a, score_a, mats_a, beside(lmat, mats_b, score_b, a + 1))
        lmat = light_rows(a)
        shade(a + 1, score_b, mats_b, beside(lmat, mats_a, score_a, jnp.minimum(a + 2, steps - 1)))

    acc[...] += dot(light_rows(steps - 1), mats_b[...], NT)
    both = acc[0:3, :] + acc[3:6, :]
    rows = [both[:, 0:PTS], both[:, PTS : 2 * PTS] + both[:, 2 * PTS : 3 * PTS]]
    for k in range(3):
        const[0, :, k : k + 1] = jnp.sum(acc_rad[k], axis=1, keepdims=True)
    rows.append(const[0].T[0:3, :])
    for j in range(sums_ref.shape[0]):
        for k in range(3):
            sums_ref[j, 3 * k : 3 * k + 3, :] = rows[k]

    @pl.loop(0, steps)
    def drain(step):
        spec_copy(step).wait()


def grad_half(
    base_tile,
    steps,
    spec_copy,
    theta_ref,
    pfs,
    nz_ref,
    azim_n,
    tfeat_ref,
    env_ref,
    energy_ref,
    out_ref,
    const,
    wmat,
    score_a,
    score_b,
    d_a,
    d_b,
    acc,
    spec_buf,
):
    first = lax.axis_index("lts") * (2 * steps) + base_tile
    mine = pl.ds(pl.multiple_of(base_tile * BLK, BLK), steps * BLK)
    out_ref[35:38, :] = energy_ref[:, mine]
    out_ref[38:40, :] = jnp.zeros((2, steps * BLK), F32)
    d_b[...] = jnp.zeros_like(d_b)

    def place(step):
        return pl.ds(pl.multiple_of(step * BLK, BLK), BLK)

    def tfeat_of(step):
        return tfeat_ref[:, place(base_tile + step)]

    def combine(step, score, d, beside):
        sin_t = theta_ref[0, first + step]
        cos_t = theta_ref[1, first + step]
        light = env_ref[:, place(base_tile + step)] * (sin_t * (0.25 * math.pi))
        spec_copy(base_tile + step).wait()

        def chunk(i, gain):
            r0 = i * CHUNK
            rows = pl.ds(r0, CHUNK)
            c = [const[k, rows, :] for k in range(6)]
            nz = nz_ref[rows, :] * cos_t
            gain = list(gain)
            for h in range(BLK // 128):
                lanes = pl.ds(h * 128, 128)
                tt = jnp.tanh(score[rows, lanes])
                lit = jnp.maximum(azim_n[rows, lanes] * sin_t + nz, 0.0)
                base = (1.0 + tt) * lit
                spec = spec_buf[base_tile + step, rows, lanes]
                total = None
                for k in range(3):
                    v = c[k] * base + c[3 + k] * spec
                    gain[3 * h + k] += fold(v)
                    lv = light[k : k + 1, 128 * h : 128 * h + 128] * v
                    total = lv if total is None else total + lv
                hi, lo = split(total * (1.0 - tt))
                d[0, rows, lanes] = hi
                d[1, rows, lanes] = lo
            return tuple(gain)

        gain = (jnp.zeros((8, 128), F32),) * 6
        for i in range(PTS // CHUNK):
            finish = beside(i)
            gain = chunk(i, gain)
            finish()
        for h in range(BLK // 128):
            for k in range(3):
                lk = light[k : k + 1, 128 * h : 128 * h + 128]
                out_ref[32 + k : 33 + k, pl.ds(pl.multiple_of(step * BLK + 128 * h, 128), 128)] = lk * jnp.sum(gain[3 * h + k], axis=0, keepdims=True)

    def contract(step, d, i):
        if i < 2:
            cols = pl.ds(128 * i, 128)
            x = dot(wmat[...], d[0, :, cols], NN)
            y = dot(wmat[0:32, :], d[1, :, cols], NN)

            def finish():
                here = pl.ds(pl.multiple_of(step * BLK + 128 * i, 128), 128)
                out_ref[0:32, here] = x[0:32] + x[32:64] + y

        else:
            t_hi, t_lo = split(tfeat_of(step))
            rows = pl.ds(128 * (i - 2), 128)
            x = dot(jnp.concatenate([t_hi, t_lo], axis=0), d[0, rows, :], NT)
            y = dot(t_hi, d[1, rows, :], NT)

            def finish():
                acc[0:32, rows] += x[0:32] + x[32:64] + y

        return finish

    def beside(step, d, score, nxt):
        t_hi, t_lo = split(tfeat_of(nxt))
        feats = jnp.concatenate([t_hi, t_hi, t_lo], axis=0)

        def run(i):
            if i in GRADS_AT:
                return contract(step, d, GRADS_AT.index(i))
            if i in SCORE_AT:
                rows = pl.ds(SCORE_AT.index(i) * SCORE_ROWS, SCORE_ROWS)
                x = dot(pfs[rows, :], feats, NN)

                def finish():
                    score[rows, :] = x

                return finish
            return lambda: None

        return run

    score_a[...] = score_tile(pfs, tfeat_of(0))

    @pl.loop(0, steps // 2)
    def pair(j):
        a = 2 * j
        combine(a, score_a, d_a, beside(jnp.maximum(a - 1, 0), d_b, score_b, a + 1))
        combine(a + 1, score_b, d_b, beside(a, d_a, score_a, jnp.minimum(a + 2, steps - 1)))

    for i in range(4):
        contract(steps - 1, d_b, i)()


def grad_kernel(
    scale,
    theta_ref,
    sums_ref,
    albedo_ref,
    observed_ref,
    pfeat_ref,
    azim_n,
    pfs,
    nz_ref,
    tfeat_ref,
    env_ref,
    spec_ref,
    energy_ref,
    rad_ref,
    galb_ref,
    grough_ref,
    gpf_ref,
    other_ref,
    own_ref,
    const,
    rbuf,
    wmat,
    score_a,
    score_b,
    d_a,
    d_b,
    acc,
    spec_buf,
    sems,
):
    tiles = tfeat_ref.shape[1] // BLK
    steps = tiles // 2
    core = lax.axis_index("pts") % 2
    half_root = 0.5 / math.sqrt(pfeat_ref.shape[0])

    def prologue():
        sums = sums_ref[0]
        for k in range(1, sums_ref.shape[0]):
            sums += sums_ref[k]
        alb = albedo_ref[...] * (1.0 / math.pi)
        radiance = scale * sums[6:9]
        resid = radiance - observed_ref[...]
        rad_ref[...] = radiance
        galb_ref[...] = (scale / math.pi) * resid * sums[0:3]
        grough_ref[...] = scale * jnp.sum(resid * sums[3:6], axis=0, keepdims=True)
        rbuf[...] = jnp.zeros_like(rbuf)
        rbuf[0:3, :] = resid * alb
        rbuf[3:6, :] = resid
        cols = rbuf[...].T
        for k in range(6):
            const[k] = jnp.broadcast_to(cols[:, k : k + 1], (PTS, 128))
        hi, lo = split(pfeat_ref[...] * half_root)
        wmat[0:32, :] = hi
        wmat[32:64, :] = lo
        acc[...] = jnp.zeros_like(acc)

    def spec_copy(tile):
        return pltpu.make_async_copy(spec_ref.at[tile], spec_buf.at[tile], sems.at[tile])

    @pl.loop(0, tiles)
    def fetch(step):
        spec_copy(lax.rem(step + (1 - core) * steps, tiles)).start()

    prologue()
    for part, out_ref in enumerate((other_ref, own_ref)):
        grad_half(
            (core if part else 1 - core) * steps, steps, spec_copy, theta_ref, pfs, nz_ref, azim_n,
            tfeat_ref, env_ref, energy_ref, out_ref, const, wmat, score_a, score_b, d_a, d_b, acc,
            spec_buf,
        )
    gpf = (scale * half_root) * acc[...]
    gpf_ref[...] = gpf


def join_kernel(own_ref, other_ref, feat_ref, light_ref):
    core = lax.axis_index("pts") % 2
    count = own_ref.shape[1]
    for x_ref, at in ((own_ref, core), (other_ref, 1 - core)):
        lanes = pl.ds(pl.multiple_of(at * count, count), count)
        feat_ref[:, lanes] = x_ref[0:32, :]
        light_ref[:, lanes] = x_ref[32:35, :]


def join(own, other, tex):
    return pl.pallas_call(
        join_kernel,
        out_shape=[jax.ShapeDtypeStruct((32, tex), F32), jax.ShapeDtypeStruct((3, tex), F32)],
        compiler_params=pltpu.CompilerParams(vmem_limit_bytes=4 * 1024 * 1024),
        name="join",
    )(own, other)


def shards(normals, view_index, cam_dirs, albedo, roughness, point_feat, observed, texel_feat, env):
    pts = normals.shape[1]
    tex = env.shape[1]
    steps = tex // BLK
    points_all = lax.axis_size("pts") * pts
    tex_all = tex * lax.axis_size("lts")
    scale = 4.0 * math.pi / tex_all
    theta = jnp.asarray(THETA_TABLE)
    phi = jnp.asarray(PHI_TABLE)

    vmem = pl.BlockSpec(memory_space=pltpu.VMEM)
    smem = pl.BlockSpec(memory_space=pltpu.SMEM)
    params = pltpu.CompilerParams(vmem_limit_bytes=20 * 1024 * 1024)

    def hbm(x):
        return pltpu.with_memory_space_constraint(x, pltpu.HBM)

    normals, cam_dirs, albedo, point_feat, observed, texel_feat, env, theta, phi = map(
        hbm, (normals, cam_dirs, albedo, point_feat, observed, texel_feat, env, theta, phi)
    )
    view_index, roughness = (hbm(x.reshape(1, pts)) for x in (view_index, roughness))

    def shape(*dims, dtype=F32):
        return jax.ShapeDtypeStruct(dims, dtype)

    spec, sums, energy, azim_n, pfs, nz = pl.pallas_call(
        shade_kernel,
        in_specs=[smem] + [vmem] * 9,
        out_specs=[pl.BlockSpec(memory_space=pl.ANY)] + [vmem] * 5,
        out_shape=[
            pltpu.HBM((steps, pts, BLK), F32),
            shape(lax.axis_size("lts"), 9, pts),
            shape(3, tex),
            shape(pts, COLS),
            shape(pts, 96, dtype=BF16),
            shape(pts, 128),
        ],
        scratch_shapes=[
            pltpu.VMEM((NCONST, PTS, 128), F32),
            pltpu.VMEM((PTS, COLS), F32),
            pltpu.VMEM((PTS, BLK), F32),
            pltpu.VMEM((PTS, BLK), F32),
            pltpu.VMEM((3 * PTS, BLK), BF16),
            pltpu.VMEM((3 * PTS, BLK), BF16),
            pltpu.VMEM((24, BLK), F32),
            pltpu.VMEM((16, 3 * PTS), F32),
            pltpu.VMEM((3, PTS, 128), F32),
            pltpu.VMEM((steps, PTS, BLK), F32),
            pltpu.SemaphoreType.DMA((steps,)),
        ],
        compiler_params=params,
        name="shade",
    )(
        theta,
        phi,
        normals,
        view_index,
        cam_dirs,
        albedo,
        roughness,
        point_feat,
        texel_feat,
        env,
    )

    def swap(x, axis, bits):
        n = lax.axis_size(axis)
        return lax.ppermute(x, axis, [(i, i ^ bits) for i in range(n)])

    spec = hbm(spec)
    sums = lax.all_to_all(sums, "lts", 0, 0)

    def grads():
        anywhere = pl.BlockSpec(memory_space=pl.ANY)
        return pl.pallas_call(
            functools.partial(grad_kernel, scale),
            in_specs=[smem] + [vmem] * 9 + [anywhere, vmem],
            out_specs=[vmem] * 6,
            out_shape=[shape(3, pts), shape(3, pts), shape(1, pts), shape(32, pts)]
            + [shape(40, tex // 2)] * 2,
            scratch_shapes=[
                pltpu.VMEM((6, PTS, 128), F32),
                pltpu.VMEM((8, PTS), F32),
                pltpu.VMEM((64, PTS), BF16),
                pltpu.VMEM((PTS, BLK), F32),
                pltpu.VMEM((PTS, BLK), F32),
                pltpu.VMEM((2, PTS, BLK), BF16),
                pltpu.VMEM((2, PTS, BLK), BF16),
                pltpu.VMEM((32, PTS), F32),
                pltpu.VMEM((steps, PTS, BLK), F32),
                pltpu.SemaphoreType.DMA((steps,)),
            ],
            compiler_params=params,
            name="grads",
        )(
            theta,
            sums,
            albedo,
            observed,
            point_feat,
            azim_n,
            pfs,
            nz,
            texel_feat,
            env,
            spec,
            energy,
        )

    place = lax.axis_index("pts")
    barrier = lax.optimization_barrier
    radiance, grad_albedo, grad_rough, gpf, other, own = grads()
    other = swap(other, "pts", 1)

    quad = tex // 8
    group = (place >> 1) & 3
    gpf_other = swap(gpf, "lts", 4)
    x = own + other
    cut = [lax.dynamic_slice(x, (0, quad * (group ^ m)), (40, quad)) for m in range(4)]
    got = [swap(cut[m], "pts", 2 * m) for m in (1, 2, 3)]
    x = (cut[0] + got[0]) + (got[1] + got[2])
    x, gpf_other = barrier((x, gpf_other))
    got = [swap(x, "pts", m) for m in (8, 16, 24)]
    gpf = gpf + gpf_other
    gpf_other = swap(gpf, "lts", 1)
    x = (x + got[0]) + (got[1] + got[2])
    light_step = x[32:35] * lax.rsqrt(x[35:38] + 1e-06 * points_all)
    total = jnp.sum(x[35:38], axis=0, keepdims=True)
    feat_step = x[0:32] * lax.rsqrt(total + 3e-06 * points_all)
    x = jnp.concatenate([feat_step, light_step], axis=0)
    x, gpf_other = barrier((x, gpf_other))
    gpf = gpf + gpf_other
    gpf_other = swap(gpf, "lts", 2)
    got = [x] + [swap(x, "pts", 2 * m) for m in (1, 2, 3)]
    pieces = []
    for j in range(4):
        k = group ^ j
        low = jnp.where(k == 0, got[0], got[1])
        pieces.append(jnp.where(k < 2, low, jnp.where(k == 2, got[2], got[3])))
    x = jnp.concatenate(pieces, axis=1)
    x, gpf_other = barrier((x, gpf_other))
    other = swap(x, "pts", 1)
    gpf = gpf + gpf_other
    feat_step, light_step = join(x, other, tex)
    return (radiance, grad_albedo, grad_rough.reshape(pts), gpf, light_step, feat_step)


def solution(mesh):
    return jax.shard_map(
        shards,
        mesh=mesh,
        in_specs=(
            P(None, "pts"),
            P("pts"),
            P(),
            P(None, "pts"),
            P("pts"),
            P(None, "pts"),
            P(None, "pts"),
            P(None, "lts"),
            P(None, "lts"),
        ),
        out_specs=(
            P(None, "pts"),
            P(None, "pts"),
            P("pts"),
            P(None, "pts"),
            P(None, "lts"),
            P(None, "lts"),
        ),
        check_vma=False,
    )
```

```python
import functools
import math

import jax
import jax.numpy as jnp
import numpy as np
from jax import lax
from jax.experimental import pallas as pl
from jax.experimental.pallas import tpu as pltpu
from jax.sharding import PartitionSpec as P

ROWS = 128
COLS = 256
F32 = jnp.float32
BF16 = jnp.bfloat16

THETA = np.pi * (np.arange(ROWS) + 0.5) / ROWS
PHI = 2.0 * np.pi * (np.arange(COLS) + 0.5) / COLS
THETA_TABLE = np.stack([np.sin(THETA), np.cos(THETA)]).astype(np.float32)
PHI_TABLE = np.stack([np.cos(PHI), np.sin(PHI)]).astype(np.float32)

PTS = 256
BLK = 256
CHUNK = 32
GRADS_AT = (0, 1, 3, 4)
SUMS_AT = (0, 1, 2, 3, 4, 5)
SUM_ROWS = 128
SCORE_AT = (6,)
SCORE_ROWS = 256
(NZ, VZ, NV0, KEEP, KOFF, C1, C0, YA, ALB) = range(9)
NCONST = 11

NT = (((1,), (1,)), ((), ()))
NN = (((1,), (0,)), ((), ()))


def dot(a, b, dims):
    return lax.dot_general(a, b, dims, preferred_element_type=F32)


def split(x):
    hi = x.astype(BF16)
    return hi, (x - hi.astype(F32)).astype(BF16)


def score_tile(pfs_ref, tfeat):
    t_hi, t_lo = split(tfeat)
    return dot(pfs_ref[...], jnp.concatenate([t_hi, t_hi, t_lo], axis=0), NN)


def fold(x):
    return (x[0:8] + x[8:16]) + (x[16:24] + x[24:32])


def shade_kernel(
    theta_ref,
    phi_ref,
    normals_ref,
    view_ref,
    cams_ref,
    albedo_ref,
    rough_ref,
    pfeat_ref,
    tfeat_in,
    env_ref,
    spec_ref,
    sums_ref,
    energy_ref,
    azim_n,
    pfs,
    nz_ref,
    tfeat_ref,
    last_ref,
    const,
    azim_s,
    azim_v,
    undo,
    score_a,
    score_b,
    mats_a,
    mats_b,
    ebuf,
    acc,
    acc_rad,
    spec_buf,
    sems,
    tfeat_sem,
):
    steps = tfeat_ref.shape[1] // BLK
    first = lax.axis_index("lts") * steps
    core = lax.axis_index("pts") % 2
    offset = (1 - core) * (steps // 2) + 2

    def tile_of(k):
        return lax.rem(k + offset, steps)


    def prologue():
        normals = normals_ref[...]
        cams = lax.broadcasted_iota(jnp.int32, (cams_ref.shape[1], PTS), 0)
        choose = (cams == view_ref[...]).astype(F32)
        views = lax.dot_general(
            cams_ref[...], choose, NN, precision=lax.Precision.HIGHEST, preferred_element_type=F32
        )
        rough = rough_ref[...]
        alpha = rough * rough
        alpha_sq = alpha * alpha
        half = 0.5 * alpha
        nv0 = jnp.sum(normals * views, axis=0, keepdims=True)
        nv = jnp.maximum(nv0, 0.1)
        geo_v = nv * (1.0 - half) + half
        lead = alpha_sq / (4.0 * math.pi * geo_v)
        y_d = -4.0 * alpha / (1.0 - alpha_sq)
        y_g = -0.5 / (1.0 - half)
        y_a = 2.0 / alpha - y_d - y_g - (1.0 - nv) / (2.0 * geo_v)
        root = 0.5 * jnp.sqrt(1.0 - alpha_sq)
        ratio = y_d / y_g
        rows = [None] * NCONST
        rows[NZ] = root * normals[2:3]
        rows[VZ] = 0.5 * views[2:3]
        rows[NV0] = root * nv0
        rows[KEEP] = ratio * (1.0 - half) / root
        rows[KOFF] = ratio * half
        rows[C1] = 0.96 * lead * ratio / root
        rows[C0] = 0.04 * lead * ratio / root
        rows[YA] = y_a / y_d
        for k in range(3):
            rows[ALB + k] = albedo_ref[k : k + 1, :] * (1.0 / math.pi) / root
        rows += [normals[0:1], normals[1:2], normals[2:3], root * normals[0:1], root * normals[1:2]]
        rows += [0.5 * views[0:1], 0.5 * views[1:2]]
        undo[0:1, :] = 1.0 / root
        undo[1:2, :] = 2.0 * rough * y_d
        ebuf[...] = jnp.zeros_like(ebuf)
        for k, r in enumerate(rows):
            ebuf[k : k + 1, :] = r
        cols = ebuf[...].T
        for k in range(NCONST):
            const[k] = jnp.broadcast_to(cols[:, k : k + 1], (PTS, 128))
        nz_ref[...] = jnp.broadcast_to(cols[:, NCONST + 2 : NCONST + 3], (PTS, 128))
        cos_p = phi_ref[0:1, :]
        sin_p = phi_ref[1:2, :]
        k = NCONST
        azim_n[...] = cols[:, k : k + 1] * cos_p + cols[:, k + 1 : k + 2] * sin_p
        azim_s[...] = cols[:, k + 3 : k + 4] * cos_p + cols[:, k + 4 : k + 5] * sin_p
        azim_v[...] = cols[:, k + 5 : k + 6] * cos_p + cols[:, k + 6 : k + 7] * sin_p
        hi, lo = split((pfeat_ref[...] * (0.5 / math.sqrt(pfeat_ref.shape[0]))).T)
        pfs[:, 0:32] = hi
        pfs[:, 32:64] = lo
        pfs[:, 64:96] = hi
        ebuf[...] = jnp.zeros_like(ebuf)
        acc[...] = jnp.zeros_like(acc)
        acc_rad[...] = jnp.zeros_like(acc_rad)

    tfeat_copy = pltpu.make_async_copy(tfeat_in, tfeat_ref, tfeat_sem)
    tfeat_copy.start()
    prologue()
    tfeat_copy.wait()
    mats_b[...] = jnp.zeros_like(mats_b)

    def place(step):
        return pl.ds(pl.multiple_of(step * BLK, BLK), BLK)

    def light_of(step):
        return env_ref[:, place(step)] * (theta_ref[0, first + step] * (0.25 * math.pi))

    def spec_copy(k):
        return pltpu.make_async_copy(spec_buf.at[k], spec_ref.at[tile_of(k)], sems.at[k])

    def shade(k_step, score, mats, beside):
        step = tile_of(k_step)
        sin_t = theta_ref[0, first + step]
        cos_t = theta_ref[1, first + step]
        light = light_of(step)

        def chunk(i, eng):
            r0 = i * CHUNK
            rows = pl.ds(r0, CHUNK)
            c = [const[k, rows, :] for k in range(NCONST)]
            nz = c[NZ] * cos_t
            vz = c[VZ] * cos_t + 0.5
            eng = list(eng)
            rad = [None] * 3
            for h in range(BLK // 128):
                lanes = pl.ds(h * 128, 128)
                nl = azim_s[rows, lanes] * sin_t + nz
                vv = azim_v[rows, lanes] * sin_t + vz
                tt = jnp.tanh(score[rows, lanes])
                lit = jnp.maximum(nl, 0.0)
                inv_len = lax.rsqrt(jnp.maximum(vv, 0.125))
                nh = (nl + c[NV0]) * inv_len
                dd = 1.0 - nh * nh
                gg = lit * c[KEEP] + c[KOFF]
                inv = pl.reciprocal(dd * dd * gg, approx=True)
                x1 = 1.0 - vv * inv_len
                x2 = x1 * x1
                fres = x2 * x2 * x1 * c[C1] + c[C0]
                base = (1.0 + tt) * lit
                spec = fres * inv * base
                fact = inv * dd * (gg + dd) + c[YA]
                spec_buf[k_step, rows, lanes] = spec
                hi, lo = split(spec * fact)
                mats[pl.ds(r0, CHUNK), lanes] = base.astype(BF16)
                mats[pl.ds(PTS + r0, CHUNK), lanes] = hi
                mats[pl.ds(2 * PTS + r0, CHUNK), lanes] = lo
                for k in range(3):
                    v = c[ALB + k] * base + spec
                    eng[3 * h + k] += fold(v * v)
                    lv = light[k : k + 1, 128 * h : 128 * h + 128] * v
                    rad[k] = lv if h == 0 else rad[k] + lv
            for k in range(3):
                acc_rad[k, rows, :] += rad[k]
            return tuple(eng)

        eng = (jnp.zeros((8, 128), F32),) * 6
        for i in range(PTS // CHUNK):
            finish = beside(i)
            eng = chunk(i, eng)
            finish()
        for h in range(BLK // 128):
            for k in range(3):
                lk = light[k : k + 1, 128 * h : 128 * h + 128]
                energy_ref[k : k + 1, pl.ds(pl.multiple_of(step * BLK + 128 * h, 128), 128)] = lk * lk * jnp.sum(eng[3 * h + k], axis=0, keepdims=True)


    def light_rows(k_step):
        light = light_of(tile_of(k_step))
        l_hi = light.astype(BF16).astype(F32)
        ebuf[0:3, :] = l_hi
        ebuf[3:6, :] = light - l_hi
        return ebuf[0:16, :].astype(BF16)

    def beside(lmat, mats, score, nxt):
        t_hi, t_lo = split(tfeat_ref[:, place(tile_of(nxt))])
        feats = jnp.concatenate([t_hi, t_hi, t_lo], axis=0)

        def run(i):
            if i in SUMS_AT:
                part = pl.ds(SUMS_AT.index(i) * SUM_ROWS, SUM_ROWS)
                x = dot(lmat, mats[part, :], NT)

                def finish():
                    acc[:, part] += x

            elif i in SCORE_AT:
                rows = pl.ds(SCORE_AT.index(i) * SCORE_ROWS, SCORE_ROWS)
                x = dot(pfs[rows, :], feats, NN)

                def finish():
                    score[rows, :] = x

            else:

                def finish():
                    pass

            return finish

        return run

    score_a[...] = score_tile(pfs, tfeat_ref[:, place(tile_of(0))])

    def pair(j):
        a = 2 * j
        lmat = light_rows(jnp.maximum(a - 1, 0))
        shade(a, score_a, mats_a, beside(lmat, mats_b, score_b, a + 1))
        lmat = light_rows(a)
        shade(a + 1, score_b, mats_b, beside(lmat, mats_a, score_a, jnp.minimum(a + 2, steps - 1)))

        @pl.when(j < steps // 2 - 1)
        def send():
            spec_copy(a).start()
            spec_copy(a + 1).start()

    pl.loop(0, steps // 2)(pair)
    acc[...] += dot(light_rows(steps - 1), mats_b[...], NT)
    both = acc[0:3, :] + acc[3:6, :]
    rows = [
        both[:, 0:PTS] * undo[0:1, :],
        (both[:, PTS : 2 * PTS] + both[:, 2 * PTS : 3 * PTS]) * undo[1:2, :],
    ]
    for k in range(3):
        const[0, :, k : k + 1] = jnp.sum(acc_rad[k], axis=1, keepdims=True)
    rows.append(const[0].T[0:3, :])
    for j in range(sums_ref.shape[0]):
        for k in range(3):
            sums_ref[j, 3 * k : 3 * k + 3, :] = rows[k]

    last_ref[...] = spec_buf[steps - 2 : steps]

    @pl.loop(0, steps - 2)
    def drain(step):
        spec_copy(step).wait()


def grad_half(
    base_tile,
    steps,
    spec_copy,
    theta_ref,
    pfs,
    nz_ref,
    azim_n,
    tfeat_ref,
    env_ref,
    energy_ref,
    out_ref,
    const,
    wmat,
    score_a,
    score_b,
    d_a,
    d_b,
    acc,
    spec_buf,
):
    first = lax.axis_index("lts") * (2 * steps) + base_tile
    mine = pl.ds(pl.multiple_of(base_tile * BLK, BLK), steps * BLK)
    out_ref[35:38, :] = energy_ref[:, mine]
    out_ref[38:40, :] = jnp.zeros((2, steps * BLK), F32)
    d_b[...] = jnp.zeros_like(d_b)

    def place(step):
        return pl.ds(pl.multiple_of(step * BLK, BLK), BLK)

    def tfeat_of(step):
        return tfeat_ref[:, place(base_tile + step)]

    def combine(step, score, d, beside):
        sin_t = theta_ref[0, first + step]
        cos_t = theta_ref[1, first + step]
        light = env_ref[:, place(base_tile + step)] * (sin_t * (0.25 * math.pi))
        spec_copy(base_tile + step).wait()

        def chunk(i, gain):
            r0 = i * CHUNK
            rows = pl.ds(r0, CHUNK)
            c = [const[k, rows, :] for k in range(6)]
            nz = nz_ref[rows, :] * cos_t
            gain = list(gain)
            for h in range(BLK // 128):
                lanes = pl.ds(h * 128, 128)
                tt = jnp.tanh(score[rows, lanes])
                lit = jnp.maximum(azim_n[rows, lanes] * sin_t + nz, 0.0)
                base = (1.0 + tt) * lit
                spec = spec_buf[base_tile + step, rows, lanes]
                total = None
                for k in range(3):
                    v = c[k] * base + c[3 + k] * spec
                    gain[3 * h + k] += fold(v)
                    lv = light[k : k + 1, 128 * h : 128 * h + 128] * v
                    total = lv if total is None else total + lv
                hi, lo = split(total * (1.0 - tt))
                d[0, rows, lanes] = hi
                d[1, rows, lanes] = lo
            return tuple(gain)

        gain = (jnp.zeros((8, 128), F32),) * 6
        for i in range(PTS // CHUNK):
            finish = beside(i)
            gain = chunk(i, gain)
            finish()
        for h in range(BLK // 128):
            for k in range(3):
                lk = light[k : k + 1, 128 * h : 128 * h + 128]
                out_ref[32 + k : 33 + k, pl.ds(pl.multiple_of(step * BLK + 128 * h, 128), 128)] = lk * jnp.sum(gain[3 * h + k], axis=0, keepdims=True)

    def contract(step, d, i):
        if i < 2:
            cols = pl.ds(128 * i, 128)
            x = dot(wmat[...], d[0, :, cols], NN)
            y = dot(wmat[0:32, :], d[1, :, cols], NN)

            def finish():
                here = pl.ds(pl.multiple_of(step * BLK + 128 * i, 128), 128)
                out_ref[0:32, here] = x[0:32] + x[32:64] + y

        else:
            t_hi, t_lo = split(tfeat_of(step))
            rows = pl.ds(128 * (i - 2), 128)
            x = dot(jnp.concatenate([t_hi, t_lo], axis=0), d[0, rows, :], NT)
            y = dot(t_hi, d[1, rows, :], NT)

            def finish():
                acc[0:32, rows] += x[0:32] + x[32:64] + y

        return finish

    def beside(step, d, score, nxt):
        t_hi, t_lo = split(tfeat_of(nxt))
        feats = jnp.concatenate([t_hi, t_hi, t_lo], axis=0)

        def run(i):
            if i in GRADS_AT:
                return contract(step, d, GRADS_AT.index(i))
            if i in SCORE_AT:
                rows = pl.ds(SCORE_AT.index(i) * SCORE_ROWS, SCORE_ROWS)
                x = dot(pfs[rows, :], feats, NN)

                def finish():
                    score[rows, :] = x

                return finish
            return lambda: None

        return run

    score_a[...] = score_tile(pfs, tfeat_of(0))

    @pl.loop(0, steps // 2)
    def pair(j):
        a = 2 * j
        combine(a, score_a, d_a, beside(jnp.maximum(a - 1, 0), d_b, score_b, a + 1))
        combine(a + 1, score_b, d_b, beside(a, d_a, score_a, jnp.minimum(a + 2, steps - 1)))

    for i in range(4):
        contract(steps - 1, d_b, i)()


def grad_kernel(
    scale,
    theta_ref,
    sums_ref,
    albedo_ref,
    observed_ref,
    pfeat_ref,
    azim_n,
    pfs,
    nz_ref,
    tfeat_ref,
    env_ref,
    spec_ref,
    energy_ref,
    last_ref,
    rad_ref,
    galb_ref,
    grough_ref,
    gpf_ref,
    other_ref,
    own_ref,
    const,
    rbuf,
    wmat,
    score_a,
    score_b,
    d_a,
    d_b,
    acc,
    spec_buf,
    sems,
):
    tiles = tfeat_ref.shape[1] // BLK
    steps = tiles // 2
    core = lax.axis_index("pts") % 2
    half_root = 0.5 / math.sqrt(pfeat_ref.shape[0])

    def prologue():
        sums = sums_ref[0]
        for k in range(1, sums_ref.shape[0]):
            sums += sums_ref[k]
        alb = albedo_ref[...] * (1.0 / math.pi)
        radiance = scale * sums[6:9]
        resid = radiance - observed_ref[...]
        rad_ref[...] = radiance
        galb_ref[...] = (scale / math.pi) * resid * sums[0:3]
        grough_ref[...] = scale * jnp.sum(resid * sums[3:6], axis=0, keepdims=True)
        rbuf[...] = jnp.zeros_like(rbuf)
        rbuf[0:3, :] = resid * alb
        rbuf[3:6, :] = resid
        cols = rbuf[...].T
        for k in range(6):
            const[k] = jnp.broadcast_to(cols[:, k : k + 1], (PTS, 128))
        hi, lo = split(pfeat_ref[...] * half_root)
        wmat[0:32, :] = hi
        wmat[32:64, :] = lo
        acc[...] = jnp.zeros_like(acc)

    def spec_copy(tile):
        return pltpu.make_async_copy(spec_ref.at[tile], spec_buf.at[tile], sems.at[tile])

    for step in range(2):
        tile = (1 - core) * steps + step
        pltpu.make_async_copy(last_ref.at[step], spec_buf.at[tile], sems.at[tile]).start()

    @pl.loop(2, tiles)
    def fetch(step):
        spec_copy(lax.rem(step + (1 - core) * steps, tiles)).start()

    prologue()
    for part, out_ref in enumerate((other_ref, own_ref)):
        grad_half(
            (core if part else 1 - core) * steps, steps, spec_copy, theta_ref, pfs, nz_ref, azim_n,
            tfeat_ref, env_ref, energy_ref, out_ref, const, wmat, score_a, score_b, d_a, d_b, acc,
            spec_buf,
        )
    gpf = (scale * half_root) * acc[...]
    gpf_ref[...] = gpf


def join_kernel(own_ref, other_ref, feat_ref, light_ref):
    core = lax.axis_index("pts") % 2
    count = own_ref.shape[1]
    for x_ref, at in ((own_ref, core), (other_ref, 1 - core)):
        lanes = pl.ds(pl.multiple_of(at * count, count), count)
        feat_ref[:, lanes] = x_ref[0:32, :]
        light_ref[:, lanes] = x_ref[32:35, :]


def join(own, other, tex):
    return pl.pallas_call(
        join_kernel,
        out_shape=[jax.ShapeDtypeStruct((32, tex), F32), jax.ShapeDtypeStruct((3, tex), F32)],
        compiler_params=pltpu.CompilerParams(vmem_limit_bytes=4 * 1024 * 1024),
        name="join",
    )(own, other)


def shards(normals, view_index, cam_dirs, albedo, roughness, point_feat, observed, texel_feat, env):
    pts = normals.shape[1]
    tex = env.shape[1]
    steps = tex // BLK
    points_all = lax.axis_size("pts") * pts
    tex_all = tex * lax.axis_size("lts")
    scale = 4.0 * math.pi / tex_all
    theta = jnp.asarray(THETA_TABLE)
    phi = jnp.asarray(PHI_TABLE)

    vmem = pl.BlockSpec(memory_space=pltpu.VMEM)
    smem = pl.BlockSpec(memory_space=pltpu.SMEM)
    anywhere = pl.BlockSpec(memory_space=pl.ANY)
    params = pltpu.CompilerParams(vmem_limit_bytes=20 * 1024 * 1024)

    def hbm(x):
        return pltpu.with_memory_space_constraint(x, pltpu.HBM)

    normals, cam_dirs, albedo, point_feat, observed, texel_feat, env, theta, phi = map(
        hbm, (normals, cam_dirs, albedo, point_feat, observed, texel_feat, env, theta, phi)
    )
    view_index, roughness = (hbm(x.reshape(1, pts)) for x in (view_index, roughness))

    def shape(*dims, dtype=F32):
        return jax.ShapeDtypeStruct(dims, dtype)

    spec, sums, energy, azim_n, pfs, nz, tfeat, last = pl.pallas_call(
        shade_kernel,
        in_specs=[smem] + [vmem] * 7 + [anywhere, vmem],
        out_specs=[anywhere] + [vmem] * 7,
        out_shape=[
            pltpu.HBM((steps, pts, BLK), F32),
            shape(lax.axis_size("lts"), 9, pts),
            shape(3, tex),
            shape(pts, COLS),
            shape(pts, 96, dtype=BF16),
            shape(pts, 128),
            shape(32, tex),
            shape(2, pts, BLK),
        ],
        scratch_shapes=[
            pltpu.VMEM((NCONST, PTS, 128), F32),
            pltpu.VMEM((PTS, COLS), F32),
            pltpu.VMEM((PTS, COLS), F32),
            pltpu.VMEM((8, PTS), F32),
            pltpu.VMEM((PTS, BLK), F32),
            pltpu.VMEM((PTS, BLK), F32),
            pltpu.VMEM((3 * PTS, BLK), BF16),
            pltpu.VMEM((3 * PTS, BLK), BF16),
            pltpu.VMEM((24, BLK), F32),
            pltpu.VMEM((16, 3 * PTS), F32),
            pltpu.VMEM((3, PTS, 128), F32),
            pltpu.VMEM((steps, PTS, BLK), F32),
            pltpu.SemaphoreType.DMA((steps,)),
            pltpu.SemaphoreType.DMA,
        ],
        compiler_params=params,
        name="shade",
    )(
        theta,
        phi,
        normals,
        view_index,
        cam_dirs,
        albedo,
        roughness,
        point_feat,
        texel_feat,
        env,
    )

    def swap(x, axis, bits):
        n = lax.axis_size(axis)
        return lax.ppermute(x, axis, [(i, i ^ bits) for i in range(n)])

    spec = hbm(spec)
    sums = lax.all_to_all(sums, "lts", 0, 0)

    def grads():
        return pl.pallas_call(
            functools.partial(grad_kernel, scale),
            in_specs=[smem] + [vmem] * 9 + [anywhere, vmem, vmem],
            out_specs=[vmem] * 6,
            out_shape=[shape(3, pts), shape(3, pts), shape(1, pts), shape(32, pts)]
            + [shape(40, tex // 2)] * 2,
            scratch_shapes=[
                pltpu.VMEM((6, PTS, 128), F32),
                pltpu.VMEM((8, PTS), F32),
                pltpu.VMEM((64, PTS), BF16),
                pltpu.VMEM((PTS, BLK), F32),
                pltpu.VMEM((PTS, BLK), F32),
                pltpu.VMEM((2, PTS, BLK), BF16),
                pltpu.VMEM((2, PTS, BLK), BF16),
                pltpu.VMEM((32, PTS), F32),
                pltpu.VMEM((steps, PTS, BLK), F32),
                pltpu.SemaphoreType.DMA((steps,)),
            ],
            compiler_params=params,
            name="grads",
        )(
            theta,
            sums,
            albedo,
            observed,
            point_feat,
            azim_n,
            pfs,
            nz,
            tfeat,
            env,
            spec,
            energy,
            last,
        )

    place = lax.axis_index("pts")
    barrier = lax.optimization_barrier
    radiance, grad_albedo, grad_rough, gpf, other, own = grads()
    other = swap(other, "pts", 1)

    quad = tex // 8
    group = (place >> 1) & 3
    gpf_other = swap(gpf, "lts", 4)
    x = own + other
    cut = [lax.dynamic_slice(x, (0, quad * (group ^ m)), (40, quad)) for m in range(4)]
    got = [swap(cut[m], "pts", 2 * m) for m in (1, 2, 3)]
    x = (cut[0] + got[0]) + (got[1] + got[2])
    x, gpf_other = barrier((x, gpf_other))
    got = [swap(x, "pts", m) for m in (8, 16, 24)]
    gpf = gpf + gpf_other
    gpf_other = swap(gpf, "lts", 1)
    x = (x + got[0]) + (got[1] + got[2])
    light_step = x[32:35] * lax.rsqrt(x[35:38] + 1e-06 * points_all)
    total = jnp.sum(x[35:38], axis=0, keepdims=True)
    feat_step = x[0:32] * lax.rsqrt(total + 3e-06 * points_all)
    x = jnp.concatenate([feat_step, light_step], axis=0)
    x, gpf_other = barrier((x, gpf_other))
    gpf = gpf + gpf_other
    gpf_other = swap(gpf, "lts", 2)
    got = [x] + [swap(x, "pts", 2 * m) for m in (1, 2, 3)]
    pieces = []
    for j in range(4):
        k = group ^ j
        low = jnp.where(k == 0, got[0], got[1])
        pieces.append(jnp.where(k < 2, low, jnp.where(k == 2, got[2], got[3])))
    x = jnp.concatenate(pieces, axis=1)
    x, gpf_other = barrier((x, gpf_other))
    other = swap(x, "pts", 1)
    gpf = gpf + gpf_other
    feat_step, light_step = join(x, other, tex)
    return (radiance, grad_albedo, grad_rough.reshape(pts), gpf, light_step, feat_step)


def solution(mesh):
    return jax.shard_map(
        shards,
        mesh=mesh,
        in_specs=(
            P(None, "pts"),
            P("pts"),
            P(),
            P(None, "pts"),
            P("pts"),
            P(None, "pts"),
            P(None, "pts"),
            P(None, "lts"),
            P(None, "lts"),
        ),
        out_specs=(
            P(None, "pts"),
            P(None, "pts"),
            P("pts"),
            P(None, "pts"),
            P(None, "lts"),
            P(None, "lts"),
        ),
        check_vma=False,
    )
```

```python
import functools
import math

import jax
import jax.numpy as jnp
import numpy as np
from jax import lax
from jax.experimental import pallas as pl
from jax.experimental.pallas import tpu as pltpu
from jax.sharding import PartitionSpec as P

ROWS = 128
COLS = 256
F32 = jnp.float32
BF16 = jnp.bfloat16

THETA = np.pi * (np.arange(ROWS) + 0.5) / ROWS
PHI = 2.0 * np.pi * (np.arange(COLS) + 0.5) / COLS
THETA_TABLE = np.stack([np.sin(THETA), np.cos(THETA)]).astype(np.float32)
PHI_TABLE = np.stack([np.cos(PHI), np.sin(PHI)]).astype(np.float32)

PTS = 256
BLK = 256
CHUNK = 32
GRADS_AT = (0, 1, 3, 4)
SUMS_AT = (0, 1, 2, 3, 4, 5)
SUM_ROWS = 128
SCORE_AT = (6,)
SCORE_ROWS = 256
(NZ, VZ, NV0, KEEP, KOFF, C1, C0, YA, ALB) = range(9)
NCONST = 11

NT = (((1,), (1,)), ((), ()))
NN = (((1,), (0,)), ((), ()))


def dot(a, b, dims):
    return lax.dot_general(a, b, dims, preferred_element_type=F32)


def split(x):
    hi = x.astype(BF16)
    return hi, (x - hi.astype(F32)).astype(BF16)


def score_tile(pfs_ref, tfeat):
    t_hi, t_lo = split(tfeat)
    return dot(pfs_ref[...], jnp.concatenate([t_hi, t_hi, t_lo], axis=0), NN)


def fold(x):
    return (x[0:8] + x[8:16]) + (x[16:24] + x[24:32])


def shade_kernel(
    theta_ref,
    phi_ref,
    normals_ref,
    view_ref,
    cams_ref,
    albedo_ref,
    rough_ref,
    pfeat_ref,
    tfeat_in,
    env_ref,
    spec_ref,
    sums_ref,
    energy_ref,
    azim_n,
    pfs,
    nz_ref,
    tfeat_ref,
    last_ref,
    const,
    azim_s,
    azim_v,
    undo,
    score_a,
    score_b,
    mats_a,
    mats_b,
    ebuf,
    acc,
    acc_rad,
    spec_buf,
    sems,
    tfeat_sem,
):
    steps = tfeat_ref.shape[1] // BLK
    first = lax.axis_index("lts") * steps
    core = lax.axis_index("pts") % 2
    offset = (1 - core) * (steps // 2) + 2

    def tile_of(k):
        return lax.rem(k + offset, steps)


    def prologue():
        normals = normals_ref[...]
        cams = lax.broadcasted_iota(jnp.int32, (cams_ref.shape[1], PTS), 0)
        choose = (cams == view_ref[...]).astype(F32)
        views = lax.dot_general(
            cams_ref[...], choose, NN, precision=lax.Precision.HIGHEST, preferred_element_type=F32
        )
        rough = rough_ref[...]
        alpha = rough * rough
        alpha_sq = alpha * alpha
        half = 0.5 * alpha
        nv0 = jnp.sum(normals * views, axis=0, keepdims=True)
        nv = jnp.maximum(nv0, 0.1)
        geo_v = nv * (1.0 - half) + half
        lead = alpha_sq / (4.0 * math.pi * geo_v)
        y_d = -4.0 * alpha / (1.0 - alpha_sq)
        y_g = -0.5 / (1.0 - half)
        y_a = 2.0 / alpha - y_d - y_g - (1.0 - nv) / (2.0 * geo_v)
        root = 0.5 * jnp.sqrt(1.0 - alpha_sq)
        ratio = y_d / y_g
        rows = [None] * NCONST
        rows[NZ] = root * normals[2:3]
        rows[VZ] = 0.5 * views[2:3]
        rows[NV0] = root * nv0
        rows[KEEP] = ratio * (1.0 - half) / root
        rows[KOFF] = ratio * half
        rows[C1] = 0.96 * lead * ratio / root
        rows[C0] = 0.04 * lead * ratio / root
        rows[YA] = y_a / y_d
        for k in range(3):
            rows[ALB + k] = albedo_ref[k : k + 1, :] * (1.0 / math.pi) / root
        rows += [normals[0:1], normals[1:2], normals[2:3], root * normals[0:1], root * normals[1:2]]
        rows += [0.5 * views[0:1], 0.5 * views[1:2]]
        undo[0:1, :] = 1.0 / root
        undo[1:2, :] = 2.0 * rough * y_d
        ebuf[...] = jnp.zeros_like(ebuf)
        for k, r in enumerate(rows):
            ebuf[k : k + 1, :] = r
        cols = ebuf[...].T
        for k in range(NCONST):
            const[k] = jnp.broadcast_to(cols[:, k : k + 1], (PTS, 128))
        nz_ref[...] = jnp.broadcast_to(cols[:, NCONST + 2 : NCONST + 3], (PTS, 128))
        cos_p = phi_ref[0:1, :]
        sin_p = phi_ref[1:2, :]
        k = NCONST
        azim_n[...] = cols[:, k : k + 1] * cos_p + cols[:, k + 1 : k + 2] * sin_p
        azim_s[...] = cols[:, k + 3 : k + 4] * cos_p + cols[:, k + 4 : k + 5] * sin_p
        azim_v[...] = cols[:, k + 5 : k + 6] * cos_p + cols[:, k + 6 : k + 7] * sin_p
        hi, lo = split((pfeat_ref[...] * (0.5 / math.sqrt(pfeat_ref.shape[0]))).T)
        pfs[:, 0:32] = hi
        pfs[:, 32:64] = lo
        pfs[:, 64:96] = hi
        ebuf[...] = jnp.zeros_like(ebuf)
        acc[...] = jnp.zeros_like(acc)
        acc_rad[...] = jnp.zeros_like(acc_rad)

    tfeat_copy = pltpu.make_async_copy(tfeat_in, tfeat_ref, tfeat_sem)
    tfeat_copy.start()
    prologue()
    tfeat_copy.wait()
    mats_b[...] = jnp.zeros_like(mats_b)

    def place(step):
        return pl.ds(pl.multiple_of(step * BLK, BLK), BLK)

    def light_of(step):
        return env_ref[:, place(step)] * (theta_ref[0, first + step] * (0.25 * math.pi))

    def spec_copy(k):
        return pltpu.make_async_copy(spec_buf.at[k], spec_ref.at[tile_of(k)], sems.at[k])

    def shade(k_step, score, mats, beside):
        step = tile_of(k_step)
        sin_t = theta_ref[0, first + step]
        cos_t = theta_ref[1, first + step]
        light = light_of(step)

        def chunk(i, eng):
            r0 = i * CHUNK
            rows = pl.ds(r0, CHUNK)
            c = [const[k, rows, :] for k in range(NCONST)]
            nz = c[NZ] * cos_t
            vz = c[VZ] * cos_t + 0.5
            eng = list(eng)
            rad = [None] * 3
            for h in range(BLK // 128):
                lanes = pl.ds(h * 128, 128)
                nl = azim_s[rows, lanes] * sin_t + nz
                vv = azim_v[rows, lanes] * sin_t + vz
                tt = jnp.tanh(score[rows, lanes])
                lit = jnp.maximum(nl, 0.0)
                inv_len = lax.rsqrt(jnp.maximum(vv, 0.125))
                nh = (nl + c[NV0]) * inv_len
                dd = 1.0 - nh * nh
                gg = lit * c[KEEP] + c[KOFF]
                inv = pl.reciprocal(dd * dd * gg, approx=True)
                x1 = 1.0 - vv * inv_len
                x2 = x1 * x1
                fres = x2 * x2 * x1 * c[C1] + c[C0]
                base = (1.0 + tt) * lit
                spec = fres * inv * base
                fact = inv * dd * (gg + dd) + c[YA]
                spec_buf[k_step, rows, lanes] = spec
                hi, lo = split(spec * fact)
                mats[pl.ds(r0, CHUNK), lanes] = base.astype(BF16)
                mats[pl.ds(PTS + r0, CHUNK), lanes] = hi
                mats[pl.ds(2 * PTS + r0, CHUNK), lanes] = lo
                for k in range(3):
                    v = c[ALB + k] * base + spec
                    eng[3 * h + k] += fold(v * v)
                    lv = light[k : k + 1, 128 * h : 128 * h + 128] * v
                    rad[k] = lv if h == 0 else rad[k] + lv
            for k in range(3):
                acc_rad[k, rows, :] += rad[k]
            return tuple(eng)

        eng = (jnp.zeros((8, 128), F32),) * 6
        for i in range(PTS // CHUNK):
            finish = beside(i)
            eng = chunk(i, eng)
            finish()
        for h in range(BLK // 128):
            for k in range(3):
                lk = light[k : k + 1, 128 * h : 128 * h + 128]
                energy_ref[k : k + 1, pl.ds(pl.multiple_of(step * BLK + 128 * h, 128), 128)] = lk * lk * jnp.sum(eng[3 * h + k], axis=0, keepdims=True)


    def light_rows(k_step):
        light = light_of(tile_of(k_step))
        l_hi = light.astype(BF16).astype(F32)
        ebuf[0:3, :] = l_hi
        ebuf[3:6, :] = light - l_hi
        return ebuf[0:16, :].astype(BF16)

    def beside(lmat, mats, score, nxt):
        t_hi, t_lo = split(tfeat_ref[:, place(tile_of(nxt))])
        feats = jnp.concatenate([t_hi, t_hi, t_lo], axis=0)

        def run(i):
            if i in SUMS_AT:
                part = pl.ds(SUMS_AT.index(i) * SUM_ROWS, SUM_ROWS)
                x = dot(lmat, mats[part, :], NT)

                def finish():
                    acc[:, part] += x

            elif i in SCORE_AT:
                rows = pl.ds(SCORE_AT.index(i) * SCORE_ROWS, SCORE_ROWS)
                x = dot(pfs[rows, :], feats, NN)

                def finish():
                    score[rows, :] = x

            else:

                def finish():
                    pass

            return finish

        return run

    score_a[...] = score_tile(pfs, tfeat_ref[:, place(tile_of(0))])

    def pair(j):
        a = 2 * j
        lmat = light_rows(jnp.maximum(a - 1, 0))
        shade(a, score_a, mats_a, beside(lmat, mats_b, score_b, a + 1))
        lmat = light_rows(a)
        shade(a + 1, score_b, mats_b, beside(lmat, mats_a, score_a, jnp.minimum(a + 2, steps - 1)))

        @pl.when(j < steps // 2 - 1)
        def send():
            spec_copy(a).start()
            spec_copy(a + 1).start()

    pl.loop(0, steps // 2)(pair)
    acc[...] += dot(light_rows(steps - 1), mats_b[...], NT)
    both = acc[0:3, :] + acc[3:6, :]
    rows = [
        both[:, 0:PTS] * undo[0:1, :],
        (both[:, PTS : 2 * PTS] + both[:, 2 * PTS : 3 * PTS]) * undo[1:2, :],
    ]
    for k in range(3):
        const[0, :, k : k + 1] = jnp.sum(acc_rad[k], axis=1, keepdims=True)
    rows.append(const[0].T[0:3, :])
    for j in range(sums_ref.shape[0]):
        for k in range(3):
            sums_ref[j, 3 * k : 3 * k + 3, :] = rows[k]

    last_ref[...] = spec_buf[steps - 2 : steps]

    @pl.loop(0, steps - 2)
    def drain(step):
        spec_copy(step).wait()


def grad_half(
    base_tile,
    steps,
    spec_copy,
    theta_ref,
    pfs,
    nz_ref,
    azim_n,
    tfeat_ref,
    env_ref,
    energy_ref,
    out_ref,
    const,
    wmat,
    score_a,
    score_b,
    d_a,
    d_b,
    acc,
    spec_buf,
):
    first = lax.axis_index("lts") * (2 * steps) + base_tile
    mine = pl.ds(pl.multiple_of(base_tile * BLK, BLK), steps * BLK)
    out_ref[35:38, :] = energy_ref[:, mine]
    out_ref[38:40, :] = jnp.zeros((2, steps * BLK), F32)
    d_b[...] = jnp.zeros_like(d_b)

    def place(step):
        return pl.ds(pl.multiple_of(step * BLK, BLK), BLK)

    def tfeat_of(step):
        return tfeat_ref[:, place(base_tile + step)]

    def combine(step, score, d, beside):
        sin_t = theta_ref[0, first + step]
        cos_t = theta_ref[1, first + step]
        light = env_ref[:, place(base_tile + step)] * (sin_t * (0.25 * math.pi))
        spec_copy(base_tile + step).wait()

        def chunk(i, gain):
            r0 = i * CHUNK
            rows = pl.ds(r0, CHUNK)
            c = [const[k, rows, :] for k in range(6)]
            nz = nz_ref[rows, :] * cos_t
            gain = list(gain)
            for h in range(BLK // 128):
                lanes = pl.ds(h * 128, 128)
                tt = jnp.tanh(score[rows, lanes])
                lit = jnp.maximum(azim_n[rows, lanes] * sin_t + nz, 0.0)
                base = (1.0 + tt) * lit
                spec = spec_buf[base_tile + step, rows, lanes]
                total = None
                for k in range(3):
                    v = c[k] * base + c[3 + k] * spec
                    gain[3 * h + k] += fold(v)
                    lv = light[k : k + 1, 128 * h : 128 * h + 128] * v
                    total = lv if total is None else total + lv
                hi, lo = split(total * (1.0 - tt))
                d[0, rows, lanes] = hi
                d[1, rows, lanes] = lo
            return tuple(gain)

        gain = (jnp.zeros((8, 128), F32),) * 6
        for i in range(PTS // CHUNK):
            finish = beside(i)
            gain = chunk(i, gain)
            finish()
        for h in range(BLK // 128):
            for k in range(3):
                lk = light[k : k + 1, 128 * h : 128 * h + 128]
                out_ref[32 + k : 33 + k, pl.ds(pl.multiple_of(step * BLK + 128 * h, 128), 128)] = lk * jnp.sum(gain[3 * h + k], axis=0, keepdims=True)

    def contract(step, d, i):
        if i < 2:
            cols = pl.ds(128 * i, 128)
            x = dot(wmat[...], d[0, :, cols], NN)
            y = dot(wmat[0:32, :], d[1, :, cols], NN)

            def finish():
                here = pl.ds(pl.multiple_of(step * BLK + 128 * i, 128), 128)
                out_ref[0:32, here] = x[0:32] + x[32:64] + y

        else:
            t_hi, t_lo = split(tfeat_of(step))
            rows = pl.ds(128 * (i - 2), 128)
            x = dot(jnp.concatenate([t_hi, t_lo], axis=0), d[0, rows, :], NT)
            y = dot(t_hi, d[1, rows, :], NT)

            def finish():
                acc[0:32, rows] += x[0:32] + x[32:64] + y

        return finish

    def beside(step, d, score, nxt):
        t_hi, t_lo = split(tfeat_of(nxt))
        feats = jnp.concatenate([t_hi, t_hi, t_lo], axis=0)

        def run(i):
            if i in GRADS_AT:
                return contract(step, d, GRADS_AT.index(i))
            if i in SCORE_AT:
                rows = pl.ds(SCORE_AT.index(i) * SCORE_ROWS, SCORE_ROWS)
                x = dot(pfs[rows, :], feats, NN)

                def finish():
                    score[rows, :] = x

                return finish
            return lambda: None

        return run

    score_a[...] = score_tile(pfs, tfeat_of(0))

    @pl.loop(0, steps // 2)
    def pair(j):
        a = 2 * j
        combine(a, score_a, d_a, beside(jnp.maximum(a - 1, 0), d_b, score_b, a + 1))
        combine(a + 1, score_b, d_b, beside(a, d_a, score_a, jnp.minimum(a + 2, steps - 1)))

    for i in range(4):
        contract(steps - 1, d_b, i)()


def grad_kernel(
    scale,
    theta_ref,
    sums_ref,
    albedo_ref,
    observed_ref,
    pfeat_ref,
    azim_n,
    pfs,
    nz_ref,
    tfeat_ref,
    env_ref,
    spec_ref,
    energy_ref,
    last_ref,
    rad_ref,
    galb_ref,
    grough_ref,
    gpf_ref,
    other_ref,
    own_ref,
    const,
    rbuf,
    wmat,
    score_a,
    score_b,
    d_a,
    d_b,
    acc,
    spec_buf,
    sems,
):
    tiles = tfeat_ref.shape[1] // BLK
    steps = tiles // 2
    core = lax.axis_index("pts") % 2
    half_root = 0.5 / math.sqrt(pfeat_ref.shape[0])

    def prologue():
        sums = sums_ref[0]
        for k in range(1, sums_ref.shape[0]):
            sums += sums_ref[k]
        alb = albedo_ref[...] * (1.0 / math.pi)
        radiance = scale * sums[6:9]
        resid = radiance - observed_ref[...]
        rad_ref[...] = radiance
        galb_ref[...] = (scale / math.pi) * resid * sums[0:3]
        grough_ref[...] = scale * jnp.sum(resid * sums[3:6], axis=0, keepdims=True)
        rbuf[...] = jnp.zeros_like(rbuf)
        rbuf[0:3, :] = resid * alb
        rbuf[3:6, :] = resid
        cols = rbuf[...].T
        for k in range(6):
            const[k] = jnp.broadcast_to(cols[:, k : k + 1], (PTS, 128))
        hi, lo = split(pfeat_ref[...] * half_root)
        wmat[0:32, :] = hi
        wmat[32:64, :] = lo
        acc[...] = jnp.zeros_like(acc)

    def spec_copy(tile):
        return pltpu.make_async_copy(spec_ref.at[tile], spec_buf.at[tile], sems.at[tile])

    for step in range(2):
        tile = (1 - core) * steps + step
        pltpu.make_async_copy(last_ref.at[step], spec_buf.at[tile], sems.at[tile]).start()

    @pl.loop(2, tiles)
    def fetch(step):
        spec_copy(lax.rem(step + (1 - core) * steps, tiles)).start()

    prologue()
    for part, out_ref in enumerate((other_ref, own_ref)):
        grad_half(
            (core if part else 1 - core) * steps, steps, spec_copy, theta_ref, pfs, nz_ref, azim_n,
            tfeat_ref, env_ref, energy_ref, out_ref, const, wmat, score_a, score_b, d_a, d_b, acc,
            spec_buf,
        )
    gpf = (scale * half_root) * acc[...]
    gpf_ref[...] = gpf


def join_kernel(own_ref, other_ref, feat_ref, light_ref):
    core = lax.axis_index("pts") % 2
    count = own_ref.shape[1]
    for x_ref, at in ((own_ref, core), (other_ref, 1 - core)):
        lanes = pl.ds(pl.multiple_of(at * count, count), count)
        feat_ref[:, lanes] = x_ref[0:32, :]
        light_ref[:, lanes] = x_ref[32:35, :]


def join(own, other, tex):
    return pl.pallas_call(
        join_kernel,
        out_shape=[jax.ShapeDtypeStruct((32, tex), F32), jax.ShapeDtypeStruct((3, tex), F32)],
        compiler_params=pltpu.CompilerParams(vmem_limit_bytes=4 * 1024 * 1024),
        name="join",
    )(own, other)


def shards(normals, view_index, cam_dirs, albedo, roughness, point_feat, observed, texel_feat, env):
    pts = normals.shape[1]
    tex = env.shape[1]
    steps = tex // BLK
    points_all = lax.axis_size("pts") * pts
    tex_all = tex * lax.axis_size("lts")
    scale = 4.0 * math.pi / tex_all
    theta = jnp.asarray(THETA_TABLE)
    phi = jnp.asarray(PHI_TABLE)

    vmem = pl.BlockSpec(memory_space=pltpu.VMEM)
    smem = pl.BlockSpec(memory_space=pltpu.SMEM)
    anywhere = pl.BlockSpec(memory_space=pl.ANY)
    params = pltpu.CompilerParams(vmem_limit_bytes=20 * 1024 * 1024)

    def hbm(x):
        return pltpu.with_memory_space_constraint(x, pltpu.HBM)

    normals, cam_dirs, albedo, point_feat, observed, texel_feat, env, theta, phi = map(
        hbm, (normals, cam_dirs, albedo, point_feat, observed, texel_feat, env, theta, phi)
    )
    view_index, roughness = (hbm(x.reshape(1, pts)) for x in (view_index, roughness))

    def shape(*dims, dtype=F32):
        return jax.ShapeDtypeStruct(dims, dtype)

    spec, sums, energy, azim_n, pfs, nz, tfeat, last = pl.pallas_call(
        shade_kernel,
        in_specs=[smem] + [vmem] * 7 + [anywhere, vmem],
        out_specs=[anywhere] + [vmem] * 7,
        out_shape=[
            pltpu.HBM((steps, pts, BLK), F32),
            shape(lax.axis_size("lts"), 9, pts),
            shape(3, tex),
            shape(pts, COLS),
            shape(pts, 96, dtype=BF16),
            shape(pts, 128),
            shape(32, tex),
            shape(2, pts, BLK),
        ],
        scratch_shapes=[
            pltpu.VMEM((NCONST, PTS, 128), F32),
            pltpu.VMEM((PTS, COLS), F32),
            pltpu.VMEM((PTS, COLS), F32),
            pltpu.VMEM((8, PTS), F32),
            pltpu.VMEM((PTS, BLK), F32),
            pltpu.VMEM((PTS, BLK), F32),
            pltpu.VMEM((3 * PTS, BLK), BF16),
            pltpu.VMEM((3 * PTS, BLK), BF16),
            pltpu.VMEM((24, BLK), F32),
            pltpu.VMEM((16, 3 * PTS), F32),
            pltpu.VMEM((3, PTS, 128), F32),
            pltpu.VMEM((steps, PTS, BLK), F32),
            pltpu.SemaphoreType.DMA((steps,)),
            pltpu.SemaphoreType.DMA,
        ],
        compiler_params=params,
        name="shade",
    )(
        theta,
        phi,
        normals,
        view_index,
        cam_dirs,
        albedo,
        roughness,
        point_feat,
        texel_feat,
        env,
    )

    def swap(x, axis, bits):
        n = lax.axis_size(axis)
        return lax.ppermute(x, axis, [(i, i ^ bits) for i in range(n)])

    spec = hbm(spec)
    sums = lax.all_to_all(sums, "lts", 0, 0)

    def grads():
        return pl.pallas_call(
            functools.partial(grad_kernel, scale),
            in_specs=[smem] + [vmem] * 9 + [anywhere, vmem, vmem],
            out_specs=[vmem] * 6,
            out_shape=[shape(3, pts), shape(3, pts), shape(1, pts), shape(32, pts)]
            + [shape(40, tex // 2)] * 2,
            scratch_shapes=[
                pltpu.VMEM((6, PTS, 128), F32),
                pltpu.VMEM((8, PTS), F32),
                pltpu.VMEM((64, PTS), BF16),
                pltpu.VMEM((PTS, BLK), F32),
                pltpu.VMEM((PTS, BLK), F32),
                pltpu.VMEM((2, PTS, BLK), BF16),
                pltpu.VMEM((2, PTS, BLK), BF16),
                pltpu.VMEM((32, PTS), F32),
                pltpu.VMEM((steps, PTS, BLK), F32),
                pltpu.SemaphoreType.DMA((steps,)),
            ],
            compiler_params=params,
            name="grads",
        )(
            theta,
            sums,
            albedo,
            observed,
            point_feat,
            azim_n,
            pfs,
            nz,
            tfeat,
            env,
            spec,
            energy,
            last,
        )

    place = lax.axis_index("pts")
    barrier = lax.optimization_barrier
    radiance, grad_albedo, grad_rough, gpf, other, own = grads()
    other = swap(other, "pts", 1)

    quad = tex // 8
    group = (place >> 1) & 3
    gpf_other = swap(gpf, "lts", 4)
    x = own + other
    cut = [lax.dynamic_slice(x, (0, quad * (group ^ m)), (40, quad)) for m in range(4)]
    got = [swap(cut[m], "pts", 2 * m) for m in (3, 2, 1)]
    x = (cut[0] + got[0]) + (got[1] + got[2])
    x, gpf_other = barrier((x, gpf_other))
    got = [swap(x, "pts", m) for m in (16, 24, 8)]
    gpf = gpf + gpf_other
    gpf_other = swap(gpf, "lts", 1)
    x = (x + got[0]) + (got[1] + got[2])
    light_step = x[32:35] * lax.rsqrt(x[35:38] + 1e-06 * points_all)
    total = jnp.sum(x[35:38], axis=0, keepdims=True)
    feat_step = x[0:32] * lax.rsqrt(total + 3e-06 * points_all)
    x = jnp.concatenate([feat_step, light_step], axis=0)
    x, gpf_other = barrier((x, gpf_other))
    gpf = gpf + gpf_other
    gpf_other = swap(gpf, "lts", 2)
    got = [x] + [swap(x, "pts", 2 * m) for m in (1, 2, 3)]
    pieces = []
    for j in range(4):
        k = group ^ j
        low = jnp.where(k == 0, got[0], got[1])
        pieces.append(jnp.where(k < 2, low, jnp.where(k == 2, got[2], got[3])))
    x = jnp.concatenate(pieces, axis=1)
    x, gpf_other = barrier((x, gpf_other))
    other = swap(x, "pts", 1)
    gpf = gpf + gpf_other
    feat_step, light_step = join(x, other, tex)
    return (radiance, grad_albedo, grad_rough.reshape(pts), gpf, light_step, feat_step)


def solution(mesh):
    return jax.shard_map(
        shards,
        mesh=mesh,
        in_specs=(
            P(None, "pts"),
            P("pts"),
            P(),
            P(None, "pts"),
            P("pts"),
            P(None, "pts"),
            P(None, "pts"),
            P(None, "lts"),
            P(None, "lts"),
        ),
        out_specs=(
            P(None, "pts"),
            P(None, "pts"),
            P("pts"),
            P(None, "pts"),
            P(None, "lts"),
            P(None, "lts"),
        ),
        check_vma=False,
    )
```
